128 devices in a mesh: section: 2 (over core), ctx: 8 (over y_hi, x), head: 8 (over z, y_lo).
Axes of the slice: x: 4, y: 4 (y_hi: 2, y_lo: 2; y = y_hi * 2 + y_lo), z: 4, core: 2. Of those that a mesh axis runs over, the one named last changes fastest.
Arguments:
- prompt_query: bfloat16 [4, 4096, 8192], P('section', 'ctx', 'head'), may hold values from -8 to 8
- prompt_key: bfloat16 [4, 4096, 1024], P('section', 'ctx', 'head'), may hold values from -8 to 8
- prompt_value: bfloat16 [4, 4096, 1024], P('section', 'ctx', 'head'), may hold values from -6 to 6
- step_query: bfloat16 [512, 8192], P(('section', 'ctx'), 'head'), may hold values from -8 to 8
- cache_key: bfloat16 [512, 1024, 1024], P(('section', 'ctx'), None, 'head'), may hold values from -8 to 8
- cache_value: bfloat16 [512, 1024, 1024], P(('section', 'ctx'), None, 'head'), may hold values from -6 to 6
- cache_length: int32 [512], P(('section', 'ctx')), may hold values from 1 to 1024
- owner_slots: int32 [16, 2], replicated, may hold values from 0 to 3, as said below
- request_slot: int32 [512], P(('section', 'ctx')), may hold values from 0 to 1
Outputs:
- prompt_context: bfloat16 [4, 4096, 8192], P('section', 'ctx', 'head')
- step_context: bfloat16 [512, 8192], P(('section', 'ctx'), 'head')
The draws below stay inside these ranges and needn't reach their ends.
Inputs may be any that keep to these rules, and one draw needn't show every extreme that they name: `owner_slots`: each row lists 2 different prompts.
All inputs are finite; a program needn't handle non-finite values.
Results may differ from the reference program's by a relative error of at most 0.015.
Values may be sent and summed in bfloat16 or wider, within the bound.
A program may use at most 128 MiB of HBM per device.

```python
import jax
import jax.numpy as jnp
from jax import lax

HEADS = 64
KV_HEADS = 8
HEAD_DIM = 128
PL = 4096
REQ_DEV = 32
MAXC = 1024
PSLOT = 2
NPROMPT = 4
OWNERS = 16
REQ = 512


def drawn_rows(key, shape, scale):
    return jnp.clip(scale * jax.random.normal(key, shape, jnp.float32), -8.0, 8.0)


def draw_prompt_key(key, part):
    key = jax.random.fold_in(key, 11)
    shape = (NPROMPT, PL, KV_HEADS * HEAD_DIM)
    values = drawn_rows(key, shape, 1.5)
    return values.astype(jnp.bfloat16)


def draw_prompt_query(key, part):
    key = jax.random.fold_in(key, 13)
    shape = (NPROMPT, PL, HEADS * HEAD_DIM)
    values = drawn_rows(key, shape, 2.0)
    return values.astype(jnp.bfloat16)


def draw_step_query(key, part):
    key = jax.random.fold_in(key, 17)
    shape = (REQ, HEADS * HEAD_DIM)
    values = drawn_rows(key, shape, 2.0)
    return values.astype(jnp.bfloat16)


def draw_cache_length(key, part):
    key = jax.random.fold_in(key, 21)
    lengths = jax.random.randint(key, (REQ,), 1, MAXC + 1, dtype=jnp.int32)
    lengths = lengths.at[0].set(MAXC)
    lengths = lengths.at[1].set(1)
    return lengths


def draw_owner_slots(key, part):
    key = jax.random.fold_in(key, 31)
    owner_keys = jax.random.split(key, OWNERS)

    def listed(owner_key):
        return jax.random.permutation(owner_key, NPROMPT)[:PSLOT].astype(jnp.int32)
    slots = jax.vmap(listed)(owner_keys)
    slots = slots.at[0].set(NPROMPT - 1 - jnp.arange(PSLOT, dtype=jnp.int32))
    slots = slots.at[OWNERS - 1].set(jnp.arange(PSLOT, dtype=jnp.int32))
    return slots


def place_ends(drawn, rng, low, largest):
    index_at = [jax.random.randint(jax.random.fold_in(rng, axis), (), 0, length) for axis, length in enumerate(drawn.shape)]
    longest = drawn.shape.index(max(drawn.shape))
    neighbour = index_at[:longest] + [(index_at[longest] + 1) % drawn.shape[longest]] + index_at[longest + 1:]
    return drawn.at[tuple(index_at)].set(low).at[tuple(neighbour)].set(largest)


def levels(own_key, dims, cuts, smallest, largest):
    loudness, own = 1.0, jax.random.fold_in(own_key, 6)
    for dim, parts in cuts:
        steps = jnp.exp(jax.random.uniform(jax.random.fold_in(own, dim), (parts,), jnp.float32, smallest / len(cuts), largest / len(cuts)))
        loudness = loudness * jnp.repeat(steps, dims[dim] // parts).reshape([-1 if axis == dim else 1 for axis in range(len(dims))])
    return loudness


def normal_values(stream_key, dims, deviation, bound, cuts=(), kind=jnp.bfloat16):
    array = deviation * jax.random.normal(stream_key, dims, jnp.float32)
    if cuts:
        array = array * levels(stream_key, dims, cuts, -0.22, 0.18)
    return jnp.clip(array, -bound, bound).astype(kind)


def setup_inputs(seed: int = 0) -> dict:
    splits = jax.random.split(jax.random.key(seed), 10)
    return {
        "prompt_query": draw_prompt_query(jax.random.fold_in(splits[9], 71), 0),
        "prompt_key": draw_prompt_key(jax.random.fold_in(splits[9], 71), 0),
        "prompt_value": normal_values(splits[2], (NPROMPT, PL, KV_HEADS * HEAD_DIM), 1.0, 6.0, ((0, 2), (1, 8), (2, 8))),
        "step_query": draw_step_query(jax.random.fold_in(splits[9], 71), 0),
        "cache_key": normal_values(splits[4], (REQ, MAXC, KV_HEADS * HEAD_DIM), 1.5, 8.0, ((0, 16), (2, 8))),
        "cache_value": normal_values(splits[5], (REQ, MAXC, KV_HEADS * HEAD_DIM), 1.0, 6.0, ((0, 16), (2, 8))),
        "cache_length": draw_cache_length(jax.random.fold_in(splits[9], 71), 0),
        "owner_slots": draw_owner_slots(jax.random.fold_in(splits[9], 71), 0),
        "request_slot": place_ends(jax.random.randint(splits[8], (REQ,), 0, PSLOT), jax.random.fold_in(splits[8], 1), 0, PSLOT - 1).astype(jnp.int32),
    }


FLOOR = -1e30


def masked_weights(scores, allowed):
    highest = jnp.max(scores, axis=-1, keepdims=True)
    weights = jnp.where(allowed, jnp.exp(scores - highest), 0.0).astype(jnp.bfloat16)
    denominator = jnp.sum(weights.astype(jnp.float32), axis=-1)
    return weights, denominator


def reference(prompt_query, prompt_key, prompt_value, step_query, cache_key, cache_value, cache_length, owner_slots, request_slot):
    group_size = HEADS // KV_HEADS
    score_scale = HEAD_DIM ** -0.5
    block_rows = min(PL, 512)
    block_count = PL // block_rows

    def prefill_block(block_index):
        prompt_index = block_index // block_count
        part_index = block_index % block_count
        query_prompt = lax.dynamic_index_in_dim(prompt_query, prompt_index, 0, keepdims=False)
        query_rows = lax.dynamic_slice_in_dim(query_prompt, part_index * block_rows, block_rows, 0)
        keys_all = lax.dynamic_index_in_dim(prompt_key, prompt_index, 0, keepdims=False).astype(jnp.float32).reshape(PL, KV_HEADS, HEAD_DIM)
        values_all = lax.dynamic_index_in_dim(prompt_value, prompt_index, 0, keepdims=False).astype(jnp.float32).reshape(PL, KV_HEADS, HEAD_DIM)
        queries = query_rows.astype(jnp.float32).reshape(block_rows, KV_HEADS, group_size, HEAD_DIM)
        scores = jnp.einsum("qkgd,nkd->kgqn", queries, keys_all) * score_scale
        query_pos = part_index * block_rows + jnp.arange(block_rows, dtype=jnp.int32)
        key_pos = jnp.arange(PL, dtype=jnp.int32)
        allowed = key_pos[None, :] <= query_pos[:, None]
        scores = jnp.where(allowed, scores, FLOOR)
        weights, denominator = masked_weights(scores, allowed)
        mixed = jnp.einsum("kgqn,nkd->kgqd", weights.astype(jnp.float32), values_all) / denominator[..., None]
        return jnp.transpose(mixed, (2, 0, 1, 3)).reshape(block_rows, HEADS * HEAD_DIM).astype(jnp.bfloat16)

    prompt_blocks = lax.map(prefill_block, jnp.arange(NPROMPT * block_count, dtype=jnp.int32))
    prompt_context = prompt_blocks.reshape(NPROMPT, PL, HEADS * HEAD_DIM)

    def decode_request(request_index):
        owner_index = request_index // REQ_DEV
        slot_index = request_slot[request_index]
        prompt_index = owner_slots[owner_index, slot_index]
        keys_all = jnp.concatenate([
            lax.dynamic_index_in_dim(prompt_key, prompt_index, 0, keepdims=False),
            lax.dynamic_index_in_dim(cache_key, request_index, 0, keepdims=False)], axis=0)
        values_all = jnp.concatenate([
            lax.dynamic_index_in_dim(prompt_value, prompt_index, 0, keepdims=False),
            lax.dynamic_index_in_dim(cache_value, request_index, 0, keepdims=False)], axis=0)
        keys_all = keys_all.astype(jnp.float32).reshape(PL + MAXC, KV_HEADS, HEAD_DIM)
        values_all = values_all.astype(jnp.float32).reshape(PL + MAXC, KV_HEADS, HEAD_DIM)
        query = lax.dynamic_index_in_dim(step_query, request_index, 0, keepdims=False)
        query = query.astype(jnp.float32).reshape(KV_HEADS, group_size, HEAD_DIM)
        scores = jnp.einsum("kgd,nkd->kgn", query, keys_all) * score_scale
        length = cache_length[request_index]
        allowed = jnp.concatenate([jnp.ones((PL,), dtype=bool), jnp.arange(MAXC, dtype=jnp.int32) < length])
        scores = jnp.where(allowed, scores, FLOOR)
        weights, denominator = masked_weights(scores, allowed)
        mixed = jnp.einsum("kgn,nkd->kgd", weights.astype(jnp.float32), values_all) / denominator[..., None]
        return mixed.reshape(HEADS * HEAD_DIM).astype(jnp.bfloat16)

    step_context = lax.map(decode_request, jnp.arange(REQ, dtype=jnp.int32))
    return prompt_context, step_context
```

```python
import jax
import jax.numpy as jnp
from jax import lax
from jax.experimental import pallas as pl
from jax.experimental.pallas import tpu as pltpu
from jax.sharding import PartitionSpec as P

HEADS = 64
KV_HEADS = 8
HEAD_DIM = 128
GROUP = HEADS // KV_HEADS
FLOOR = -1e30
SCALE2 = 1.4426950408889634 / HEAD_DIM**0.5
MESH = pl.DeviceIdType.MESH
CTX = 8
XS = 4
BLOCK = 512
REQS = 32
MAXC = 1024
CACHE_GROUP = 8
AUG = HEAD_DIM + 16

N_SENDS = 6 + 2 + 4 + 2 + 16


def dot_t(a, b):
    return lax.dot_general(a, b, (((1,), (1,)), ((), ())), preferred_element_type=jnp.float32)


def dot(a, b):
    return lax.dot_general(a, b, (((1,), (0,)), ((), ())), preferred_element_type=jnp.float32)


def split_scaled(q):
    scaled = q.astype(jnp.float32) * SCALE2
    high = scaled.astype(jnp.bfloat16)
    low = (scaled - high.astype(jnp.float32)).astype(jnp.bfloat16)
    return jnp.concatenate([high, low], axis=1)


def twice(k):
    return jnp.concatenate([k, k], axis=1)


def with_ones(v):
    return jnp.concatenate([v.T, jnp.ones((AUG - HEAD_DIM, v.shape[0]), v.dtype)], axis=0)


def kernel(
    pq, pk, pv, sq, ck, cv, lengths, owner_slots, request_slot,
    out, step_out,
    kv, q_in, q_split, acc, top, out_v, cache_k, cache_v, sq_in, sq_rows,
    c_out, c_top, c_sum, p_acc, p_top, step_v,
    send_sem, recv_sem, sib_sem, in_sem, cache_sem, out_sem,
):
    section = lax.axis_index("section")
    me = lax.axis_index("ctx")
    y, x = me // XS, lax.rem(me, XS)
    first = section * 2

    def at(row, col):
        return row * XS + lax.rem(col + XS, XS)

    left, right = at(y, x - 1), at(y, x + 1)
    across, opposite = at(1 - y, x), at(y, x + 2)
    far_left, far_right, far_opposite = at(1 - y, x - 1), at(1 - y, x + 1), at(1 - y, x + 2)
    owner = section * CTX + me

    loads = [
        pltpu.make_async_copy(pk, kv.at[0, pl.ds(first, 2), me], in_sem.at[0]),
        pltpu.make_async_copy(pv, kv.at[1, pl.ds(first, 2), me], in_sem.at[1]),
        pltpu.make_async_copy(sq, sq_in, in_sem.at[2]),
        pltpu.make_async_copy(pq, q_in, in_sem.at[3]),
    ]
    for load in loads:
        load.start()

    def cache_copies(g):
        rows = pl.ds(g * CACHE_GROUP, CACHE_GROUP)
        return (
            pltpu.make_async_copy(ck.at[rows], cache_k.at[rows], cache_sem.at[0, g]),
            pltpu.make_async_copy(cv.at[rows], cache_v.at[rows], cache_sem.at[1, g]),
        )

    for g in range(REQS // CACHE_GROUP):
        for copy in cache_copies(g):
            copy.start()

    barrier = pltpu.get_barrier_semaphore()
    for peer in (left, right, across):
        pl.semaphore_signal(barrier, inc=1, device_id={"ctx": peer}, device_id_type=MESH)
    pl.semaphore_signal(barrier, inc=1, device_id={"section": 1 - section}, device_id_type=MESH)
    pl.semaphore_wait(barrier, 4)

    def block_of(part, j):
        return kv.at[part, pl.ds(first, 2), j]

    def move(slot, part, j, to, src=None):
        return pltpu.make_async_remote_copy(
            src_ref=block_of(part, j) if src is None else src,
            dst_ref=block_of(part, j),
            send_sem=send_sem.at[slot],
            recv_sem=recv_sem.at[part, j],
            device_id={"ctx": to},
            device_id_type=MESH,
        )

    def share(slot, part, j, src=None):
        return pltpu.make_async_remote_copy(
            src_ref=block_of(part, j) if src is None else src,
            dst_ref=block_of(part, j),
            send_sem=send_sem.at[slot],
            recv_sem=sib_sem.at[part, j],
            device_id={"section": 1 - section},
            device_id_type=MESH,
        )

    def shared(part, j):
        other = kv.at[part, pl.ds(2 - first, 2), j]
        return pltpu.make_async_remote_copy(
            src_ref=other, dst_ref=other, send_sem=send_sem.at[0], recv_sem=sib_sem.at[part, j],
            device_id={"section": 1 - section}, device_id_type=MESH,
        )

    def send(copy):
        copy.start()

    for part, src in ((0, pk), (1, pv)):
        for n, to in enumerate((left, right, across)):
            send(move(part * 3 + n, part, me, to, src))
    send(share(14, 0, me, pk))
    send(share(15, 1, me, pv))

    def arrive(part, j):
        move(0, part, j, me).wait_recv()

    loads[3].wait()

    def split_step(n, _):
        p, h = n // GROUP, lax.rem(n, GROUP)
        cols = pl.ds(pl.multiple_of(h * HEAD_DIM, HEAD_DIM), HEAD_DIM)
        q_split[p, h] = split_scaled(q_in[p, :, cols])
        return 0

    lax.fori_loop(0, 2 * GROUP, split_step, 0)

    loads[2].wait()
    for h in range(GROUP):
        sq_rows[:, h, :] = sq_in[:, h * HEAD_DIM : (h + 1) * HEAD_DIM].astype(jnp.float32)

    def cache_step(g, _):
        for copy in cache_copies(g):
            copy.wait()
        scores = []
        for u in range(CACHE_GROUP):
            r = g * CACHE_GROUP + u
            scores.append(dot_t(sq_rows[r].astype(jnp.bfloat16), cache_k[r]))
        for u in range(CACHE_GROUP):
            r = g * CACHE_GROUP + u
            column = lax.broadcasted_iota(jnp.int32, (GROUP, MAXC), 1)
            s = jnp.where(column < lengths[r], scores[u], FLOOR)
            highest = jnp.max(s, axis=1, keepdims=True)
            w = jnp.exp2((s - highest) * SCALE2).astype(jnp.bfloat16)
            total = jnp.sum(w.astype(jnp.float32), axis=1, keepdims=True)
            c_out[r] = dot(w, cache_v[r])
            c_top[r] = jnp.broadcast_to(highest * SCALE2, (GROUP, HEAD_DIM))
            c_sum[r] = jnp.broadcast_to(total, (GROUP, HEAD_DIM))
        return 0

    lax.fori_loop(0, REQS // CACHE_GROUP, cache_step, 0)

    for part in (0, 1):
        loads[part].wait()
    for n, j in enumerate((left, right, across)):
        arrive(0, j)
    send(move(6, 0, left, right))
    send(move(8, 0, across, left))
    send(move(9, 0, across, right))
    for n, j in enumerate((left, right, across)):
        send(share(16 + n, 0, j))

    def diagonal_step(p, _):
        keys = twice(kv[0, first + p, me])
        values = with_ones(kv[1, first + p, me])
        key_at = lax.broadcasted_iota(jnp.int32, (BLOCK, BLOCK), 0)
        query_at = lax.broadcasted_iota(jnp.int32, (BLOCK, BLOCK), 1)
        scores = [dot_t(keys, q_split[p, h]) for h in range(GROUP)]
        for h in range(GROUP):
            s = jnp.where(key_at <= query_at, scores[h], FLOOR)
            highest = jnp.max(s, axis=0, keepdims=True)
            w = jnp.exp2(s - highest).astype(jnp.bfloat16)
            acc[p, h] = dot(values, w)
            top[p, h : h + 1, :] = highest
        return 0

    lax.fori_loop(0, 2, diagonal_step, 0)

    for j in (left, right, across):
        arrive(1, j)
    send(move(7, 1, right, left))
    send(move(10, 1, across, left))
    send(move(11, 1, across, right))
    for n, j in enumerate((left, right, across)):
        send(share(19 + n, 1, j))

    order = (left, right, across, opposite, far_left, far_right, far_opposite)

    def main_step(n, _):
        k, p = n // 2, lax.rem(n, 2)

        @pl.when(n == 2)
        def _():
            for part in (0, 1):
                arrive(part, opposite)
                send(move(12 + part, part, opposite, across))
                send(share(22 + part, part, opposite))

        @pl.when(n == 8)
        def _():
            for m, j in enumerate((far_left, far_right)):
                for part in (0, 1):
                    arrive(part, j)
                    send(share(24 + 2 * m + part, part, j))

        @pl.when(n == 12)
        def _():
            for part in (0, 1):
                arrive(part, far_opposite)
                send(share(28 + part, part, far_opposite))

        j = order[0]
        for m in range(1, len(order)):
            j = jnp.where(k == m, order[m], j)

        @pl.when(j < me)
        def _():
            keys = twice(kv[0, first + p, j])
            values = with_ones(kv[1, first + p, j])
            scores = [dot_t(keys, q_split[p, h]) for h in range(GROUP)]
            for h in range(GROUP):
                s = scores[h]
                before = top[p, h : h + 1, :]
                highest = jnp.maximum(before, jnp.max(s, axis=0, keepdims=True))
                w = jnp.exp2(s - highest).astype(jnp.bfloat16)
                acc[p, h] = acc[p, h] * jnp.exp2(before - highest) + dot(values, w)
                top[p, h : h + 1, :] = highest

        return 0

    lax.fori_loop(0, 2 * len(order), main_step, 0)

    def finish_step(n, _):
        p, h = n // GROUP, lax.rem(n, GROUP)
        a = acc[p, h]
        cols = pl.ds(pl.multiple_of(h * HEAD_DIM, HEAD_DIM), HEAD_DIM)
        out_v[p, :, cols] = (a[:HEAD_DIM] / a[HEAD_DIM : HEAD_DIM + 1]).T.astype(jnp.bfloat16)
        return 0

    lax.fori_loop(0, 2 * GROUP, finish_step, 0)
    out_copy = pltpu.make_async_copy(out_v, out, out_sem.at[0])
    out_copy.start()

    for part in (0, 1):
        for j in range(CTX):
            shared(part, j).wait_recv()
    step_q = jnp.concatenate(
        [split_scaled(sq_in[:, h * HEAD_DIM : (h + 1) * HEAD_DIM]) for h in range(GROUP)], axis=0
    )
    width = GROUP * REQS
    request = lax.rem(lax.broadcasted_iota(jnp.int32, (1, width), 1), REQS)
    slot = jnp.zeros((1, width), jnp.int32)
    for r in range(REQS):
        slot = jnp.where(request == r, request_slot[r], slot)
    second = slot == 1
    in_second = second.astype(jnp.bfloat16)
    in_first = (1.0 - second.astype(jnp.float32)).astype(jnp.bfloat16)
    prompts = (owner_slots[owner, 0], owner_slots[owner, 1])
    p_acc[...] = jnp.zeros_like(p_acc)
    p_top[...] = jnp.full(p_top.shape, FLOOR, jnp.float32)

    def persona_step(i, _):
        scores = []
        for u in range(2):
            j = i * 2 + u
            a = dot_t(twice(kv[0, prompts[0], j]), step_q)
            b = dot_t(twice(kv[0, prompts[1], j]), step_q)
            scores.append(jnp.where(second, b, a))
        before = p_top[0:1, :]
        highest = before
        for s in scores:
            highest = jnp.maximum(highest, jnp.max(s, axis=0, keepdims=True))
        total = p_acc[...] * jnp.exp2(before - highest)
        for u in range(2):
            j = i * 2 + u
            w = jnp.exp2(scores[u] - highest).astype(jnp.bfloat16)
            total = total + dot(with_ones(kv[1, prompts[0], j]), w * in_first)
            total = total + dot(with_ones(kv[1, prompts[1], j]), w * in_second)
        p_acc[...] = total
        p_top[0:1, :] = highest
        return 0

    lax.fori_loop(0, CTX // 2, persona_step, 0)

    def rows(ref):
        return jnp.concatenate([ref[:, h, :] for h in range(GROUP)], axis=0)

    def spread(row):
        return jnp.broadcast_to(row, (HEAD_DIM, width)).T

    total_p, top_p = spread(p_acc[HEAD_DIM : HEAD_DIM + 1, :]), spread(p_top[0:1, :])
    top_c = rows(c_top)
    highest = jnp.maximum(top_p, top_c)
    weight_p, weight_c = jnp.exp2(top_p - highest), jnp.exp2(top_c - highest)
    mixed = p_acc[:HEAD_DIM, :].T * weight_p + rows(c_out) * weight_c
    mixed = mixed / (total_p * weight_p + rows(c_sum) * weight_c)
    for h in range(GROUP):
        step_v[:, h * HEAD_DIM : (h + 1) * HEAD_DIM] = mixed[h * REQS : (h + 1) * REQS].astype(
            jnp.bfloat16
        )
    step_copy = pltpu.make_async_copy(step_v, step_out, out_sem.at[1])
    step_copy.start()

    for sent in range(N_SENDS):
        move(sent, 0, me, left).wait_send()
    out_copy.wait()
    step_copy.wait()


def on_device(pq, pk, pv, sq, ck, cv, lengths, owner_slots, request_slot):
    anywhere = pl.BlockSpec(memory_space=pl.ANY)
    scalars = pl.BlockSpec(memory_space=pltpu.SMEM)
    f32, bf16 = jnp.float32, jnp.bfloat16
    return pl.pallas_call(
        kernel,
        out_shape=(
            jax.ShapeDtypeStruct(pq.shape, bf16),
            jax.ShapeDtypeStruct(sq.shape, bf16),
        ),
        in_specs=[anywhere] * 6 + [scalars] * 3,
        out_specs=(anywhere, anywhere),
        scratch_shapes=[
            pltpu.VMEM((2, 4, CTX, BLOCK, HEAD_DIM), bf16),
            pltpu.VMEM(pq.shape, bf16),
            pltpu.VMEM((2, GROUP, BLOCK, 2 * HEAD_DIM), bf16),
            pltpu.VMEM((2, GROUP, AUG, BLOCK), f32),
            pltpu.VMEM((2, GROUP, BLOCK), f32),
            pltpu.VMEM(pq.shape, bf16),
            pltpu.VMEM(ck.shape, bf16),
            pltpu.VMEM(cv.shape, bf16),
            pltpu.VMEM(sq.shape, bf16),
            pltpu.VMEM((REQS, GROUP, HEAD_DIM), f32),
            pltpu.VMEM((REQS, GROUP, HEAD_DIM), f32),
            pltpu.VMEM((REQS, GROUP, HEAD_DIM), f32),
            pltpu.VMEM((REQS, GROUP, HEAD_DIM), f32),
            pltpu.VMEM((AUG, GROUP * REQS), f32),
            pltpu.VMEM((8, GROUP * REQS), f32),
            pltpu.VMEM(sq.shape, bf16),
            pltpu.SemaphoreType.DMA((N_SENDS,)),
            pltpu.SemaphoreType.DMA((2, CTX)),
            pltpu.SemaphoreType.DMA((2, CTX)),
            pltpu.SemaphoreType.DMA((4,)),
            pltpu.SemaphoreType.DMA((2, REQS // CACHE_GROUP)),
            pltpu.SemaphoreType.DMA((2,)),
        ],
        compiler_params=pltpu.CompilerParams(
            collective_id=0, has_side_effects=True, vmem_limit_bytes=60 << 20
        ),
        cost_estimate=pl.CostEstimate(
            flops=18_000_000_000, bytes_accessed=24 << 20, transcendentals=34_000_000
        ),
        name="prompt_and_step",
    )(pq, pk, pv, sq, ck, cv, lengths, owner_slots, request_slot)


def solution(mesh):
    in_specs = (
        P("section", "ctx", "head"),
        P("section", "ctx", "head"),
        P("section", "ctx", "head"),
        P(("section", "ctx"), "head"),
        P(("section", "ctx"), None, "head"),
        P(("section", "ctx"), None, "head"),
        P(("section", "ctx")),
        P(),
        P(("section", "ctx")),
    )
    out_specs = (P("section", "ctx", "head"), P(("section", "ctx"), "head"))
    return jax.shard_map(
        on_device, mesh=mesh, in_specs=in_specs, out_specs=out_specs, check_vma=False
    )
```

```python
import jax
import jax.numpy as jnp
from jax import lax
from jax.experimental import pallas as pl
from jax.experimental.pallas import tpu as pltpu
from jax.sharding import PartitionSpec as P

HEADS = 64
KV_HEADS = 8
HEAD_DIM = 128
GROUP = HEADS // KV_HEADS
FLOOR = -1e30
SCALE2 = 1.4426950408889634 / HEAD_DIM**0.5
MESH = pl.DeviceIdType.MESH
CTX = 8
XS = 4
BLOCK = 512
REQS = 32
MAXC = 1024
CACHE_GROUP = 8
AUG = HEAD_DIM + 16

HALF = GROUP // 2
PARTNER = CTX // 2

N_SENDS = 6 + 2 + 4 + 2 + 16


def dot_t(a, b):
    return lax.dot_general(a, b, (((1,), (1,)), ((), ())), preferred_element_type=jnp.float32)


def dot(a, b):
    return lax.dot_general(a, b, (((1,), (0,)), ((), ())), preferred_element_type=jnp.float32)


def split_scaled(q):
    scaled = q.astype(jnp.float32) * SCALE2
    high = scaled.astype(jnp.bfloat16)
    low = (scaled - high.astype(jnp.float32)).astype(jnp.bfloat16)
    return jnp.concatenate([high, low], axis=1)


def twice(k):
    return jnp.concatenate([k, k], axis=1)


def with_ones(v):
    return jnp.concatenate([v.T, jnp.ones((AUG - HEAD_DIM, v.shape[0]), v.dtype)], axis=0)


def kernel(
    pq, pk, pv, sq, ck, cv, lengths, owner_slots, request_slot,
    out, step_out,
    kv, q_in, q_far, q_split, acc, top, out_v, out_far, cache_k, cache_v, sq_in, sq_rows,
    c_out, c_top, c_sum, p_acc, p_top, step_v,
    send_sem, recv_sem, sib_sem, far_sem, in_sem, cache_sem, out_sem,
):
    section = lax.axis_index("section")
    me = lax.axis_index("ctx")
    y, x = me // XS, lax.rem(me, XS)
    first = section * 2
    heavy = me >= PARTNER

    def at(row, col):
        return row * XS + lax.rem(col + XS, XS)

    left, right = at(y, x - 1), at(y, x + 1)
    across, opposite = at(1 - y, x), at(y, x + 2)
    far_left, far_right, far_opposite = at(1 - y, x - 1), at(1 - y, x + 1), at(1 - y, x + 2)
    owner = section * CTX + me

    loads = []
    for p in (0, 1):
        for part, src in ((0, pk), (1, pv)):
            loads.append(
                pltpu.make_async_copy(src.at[p], kv.at[first + p, me, part], in_sem.at[len(loads)])
            )
    loads.append(pltpu.make_async_copy(pq, q_in, in_sem.at[4]))
    loads.append(pltpu.make_async_copy(sq, sq_in, in_sem.at[5]))
    for load in loads:
        load.start()

    def cache_copies(g):
        rows = pl.ds(g * CACHE_GROUP, CACHE_GROUP)
        return (
            pltpu.make_async_copy(ck.at[rows], cache_k.at[rows], cache_sem.at[0, g]),
            pltpu.make_async_copy(cv.at[rows], cache_v.at[rows], cache_sem.at[1, g]),
        )

    for g in range(REQS // CACHE_GROUP):
        for copy in cache_copies(g):
            copy.start()

    barrier = pltpu.get_barrier_semaphore()
    for peer in (left, right, across):
        pl.semaphore_signal(barrier, inc=1, device_id={"ctx": peer}, device_id_type=MESH)
    pl.semaphore_signal(barrier, inc=1, device_id={"section": 1 - section}, device_id_type=MESH)
    pl.semaphore_wait(barrier, 4)

    def move(slot, p, j, to):
        return pltpu.make_async_remote_copy(
            src_ref=kv.at[first + p, j],
            dst_ref=kv.at[first + p, j],
            send_sem=send_sem.at[slot],
            recv_sem=recv_sem.at[p, j],
            device_id={"ctx": to},
            device_id_type=MESH,
        )

    def share(n, p, j):
        return pltpu.make_async_remote_copy(
            src_ref=kv.at[first + p, j],
            dst_ref=kv.at[first + p, j],
            send_sem=send_sem.at[14 + 2 * n + p],
            recv_sem=sib_sem.at[p, j],
            device_id={"section": 1 - section},
            device_id_type=MESH,
        )

    def shared(p, j):
        other = kv.at[2 - first + p, j]
        return pltpu.make_async_remote_copy(
            src_ref=other, dst_ref=other, send_sem=send_sem.at[0], recv_sem=sib_sem.at[p, j],
            device_id={"section": 1 - section}, device_id_type=MESH,
        )

    far_cols = pl.ds(HALF * HEAD_DIM, HALF * HEAD_DIM)
    lend = pltpu.make_async_remote_copy(
        src_ref=pq.at[1, :, far_cols], dst_ref=q_far, send_sem=far_sem.at[0], recv_sem=far_sem.at[1],
        device_id={"ctx": across}, device_id_type=MESH,
    )
    give_back = pltpu.make_async_remote_copy(
        src_ref=out_far, dst_ref=out.at[1, :, far_cols], send_sem=far_sem.at[2],
        recv_sem=far_sem.at[3], device_id={"ctx": across}, device_id_type=MESH,
    )

    for p in (0, 1):
        loads[2 * p].wait()
        loads[2 * p + 1].wait()
        for n, to in enumerate((left, right, across)):
            move(p * 3 + n, p, me, to).start()

    @pl.when(heavy)
    def _():
        lend.start()

    for p in (0, 1):
        share(0, p, me).start()

    def arrive(p, j):
        move(0, p, j, me).wait_recv()

    def first_arrivals():
        for n, j in enumerate((left, right, across)):
            arrive(0, j)
        move(6, 0, left, right).start()
        move(8, 0, across, right).start()
        for n, j in enumerate((left, right, across)):
            share(1 + n, 0, j).start()

    def second_arrivals():
        for j in (left, right, across):
            arrive(1, j)
        move(7, 1, right, left).start()
        move(9, 0, across, left).start()
        move(10, 1, across, left).start()
        move(11, 1, across, right).start()
        for n, j in enumerate((left, right, across)):
            share(1 + n, 1, j).start()

    def opposite_arrives():
        for p in (0, 1):
            arrive(p, opposite)
            move(12 + p, p, opposite, across).start()
            share(4, p, opposite).start()

    def far_sides_arrive():
        for p in (0, 1):
            for n, j in enumerate((far_left, far_right)):
                arrive(p, j)
                share(5 + n, p, j).start()

    def far_opposite_arrives():
        for p in (0, 1):
            arrive(p, far_opposite)
            share(7, p, far_opposite).start()

    def split_step(n, _):
        g, u = n // HALF, lax.rem(n, HALF)
        h = lax.rem(n, GROUP)
        cols = pl.ds(pl.multiple_of(h * HEAD_DIM, HEAD_DIM), HEAD_DIM)
        q_split[g, u] = split_scaled(q_in[g // 2, :, cols])
        return 0

    loads[4].wait()
    lax.fori_loop(0, jnp.where(heavy, 3 * HALF, 4 * HALF), split_step, 0)

    def diagonal_step(p, _):
        keys = twice(kv[first + p, me, 0])
        values = with_ones(kv[first + p, me, 1])
        key_at = lax.broadcasted_iota(jnp.int32, (BLOCK, BLOCK), 0)
        query_at = lax.broadcasted_iota(jnp.int32, (BLOCK, BLOCK), 1)
        scores = [dot_t(keys, q_split[2 * p + h // HALF, h % HALF]) for h in range(GROUP)]
        for h in range(GROUP):
            g, u = 2 * p + h // HALF, h % HALF
            s = jnp.where(key_at <= query_at, scores[h], FLOOR)
            highest = jnp.max(s, axis=0, keepdims=True)
            w = jnp.exp2(s - highest).astype(jnp.bfloat16)
            acc[g, u] = dot(values, w)
            top[g, u : u + 1, :] = highest
        return 0

    lax.fori_loop(0, jnp.where(heavy, 1, 2), diagonal_step, 0)

    loads[5].wait()
    for h in range(GROUP):
        sq_rows[:, h, :] = sq_in[:, h * HEAD_DIM : (h + 1) * HEAD_DIM].astype(jnp.float32)

    def cache_step(g, _):
        @pl.when(g == 2)
        def _():
            first_arrivals()

        for copy in cache_copies(g):
            copy.wait()
        scores = []
        for u in range(CACHE_GROUP):
            r = g * CACHE_GROUP + u
            scores.append(dot_t(sq_rows[r].astype(jnp.bfloat16), cache_k[r]))
        for u in range(CACHE_GROUP):
            r = g * CACHE_GROUP + u
            column = lax.broadcasted_iota(jnp.int32, (GROUP, MAXC), 1)
            s = jnp.where(column < lengths[r], scores[u], FLOOR)
            highest = jnp.max(s, axis=1, keepdims=True)
            w = jnp.exp2((s - highest) * SCALE2).astype(jnp.bfloat16)
            total = jnp.sum(w.astype(jnp.float32), axis=1, keepdims=True)
            c_out[r] = dot(w, cache_v[r])
            c_top[r] = jnp.broadcast_to(highest * SCALE2, (GROUP, HEAD_DIM))
            c_sum[r] = jnp.broadcast_to(total, (GROUP, HEAD_DIM))
        return 0

    lax.fori_loop(0, REQS // CACHE_GROUP, cache_step, 0)

    def attend(p, j, tasks, shift=None):
        keys = twice(kv[first + p, j, 0])
        values = with_ones(kv[first + p, j, 1])
        scores = [dot_t(keys, q_split[g, u]) for g, u in tasks]
        if shift is not None:
            key_at = lax.broadcasted_iota(jnp.int32, (BLOCK, BLOCK), 0)
            query_at = lax.broadcasted_iota(jnp.int32, (BLOCK, BLOCK), 1)
            allowed = key_at - query_at <= shift
        for (g, u), s in zip(tasks, scores):
            if shift is not None:
                s = jnp.where(allowed, s, FLOOR)
            before = top[g, u : u + 1, :]
            highest = jnp.maximum(before, jnp.max(s, axis=0, keepdims=True))
            w = jnp.exp2(s - highest).astype(jnp.bfloat16)
            acc[g, u] = acc[g, u] * jnp.exp2(before - highest) + dot(values, w)
            top[g, u : u + 1, :] = highest

    alone = jnp.where(heavy, 2, 4)
    for u in range(HALF):
        acc[alone, u] = jnp.zeros((AUG, BLOCK), jnp.float32)
    top[alone] = jnp.full((HALF, BLOCK), FLOOR, jnp.float32)

    order = (left, right, across, opposite, far_left, far_right, far_opposite)

    def block_at(k):
        j = order[0]
        for m in range(1, len(order)):
            j = jnp.where(k == m, order[m], j)
        return j

    def main_step(n, _):
        k = jnp.where(n < 4, lax.rem(n, 2), n // 2)
        p = jnp.where(n < 4, n // 2, lax.rem(n, 2))

        @pl.when(n == 2)
        def _():
            second_arrivals()

        @pl.when(n == 5)
        def _():
            opposite_arrives()

        @pl.when(jnp.logical_and(heavy, n == 8))
        def _():
            far_sides_arrive()

        @pl.when(jnp.logical_and(heavy, n == 12))
        def _():
            far_opposite_arrives()

        j = block_at(k)
        whole = jnp.logical_or(p == 0, jnp.logical_not(heavy))

        @pl.when(jnp.logical_and(j < me, whole))
        def _():
            attend(p, j, [(2 * p + h // HALF, h % HALF) for h in range(GROUP)])

        @pl.when(jnp.logical_and(j < me, jnp.logical_not(whole)))
        def _():
            attend(1, j, [(2, u) for u in range(HALF)])

        return 0

    lax.fori_loop(0, 2 * len(order), main_step, 0)

    @pl.when(jnp.logical_not(heavy))
    def _():
        lend.wait_recv()

        def split_far(u, _):
            cols = pl.ds(pl.multiple_of(u * HEAD_DIM, HEAD_DIM), HEAD_DIM)
            q_split[4, u] = split_scaled(q_far[:, cols])
            return 0

        lax.fori_loop(0, HALF, split_far, 0)

    def alone_step(n, _):
        @pl.when(n == 5)
        def _():
            far_sides_arrive()

        @pl.when(n == 7)
        def _():
            far_opposite_arrives()

        j = jnp.where(n == 0, me, block_at(n - 1))
        query_block = jnp.where(heavy, me, me + PARTNER)

        @pl.when(j <= query_block)
        def _():
            attend(1, j, [(alone, u) for u in range(HALF)], (query_block - j) * BLOCK)

        return 0

    lax.fori_loop(0, jnp.where(heavy, 1, 1 + len(order)), alone_step, 0)

    def result(g, u):
        a = acc[g, u]
        return (a[:HEAD_DIM] / a[HEAD_DIM : HEAD_DIM + 1]).T.astype(jnp.bfloat16)

    @pl.when(jnp.logical_not(heavy))
    def _():
        def finish_far(u, _):
            cols = pl.ds(pl.multiple_of(u * HEAD_DIM, HEAD_DIM), HEAD_DIM)
            out_far[:, cols] = result(4, u)
            return 0

        lax.fori_loop(0, HALF, finish_far, 0)
        give_back.start()

    def finish_step(n, _):
        g, u = n // HALF, lax.rem(n, HALF)
        cols = pl.ds(pl.multiple_of(lax.rem(n, GROUP) * HEAD_DIM, HEAD_DIM), HEAD_DIM)
        out_v[g // 2, :, cols] = result(g, u)
        return 0

    lax.fori_loop(0, jnp.where(heavy, 3 * HALF, 4 * HALF), finish_step, 0)
    near_cols = pl.ds(0, HALF * HEAD_DIM)
    out_copies = (
        pltpu.make_async_copy(out_v.at[0], out.at[0], out_sem.at[0]),
        pltpu.make_async_copy(out_v.at[1, :, near_cols], out.at[1, :, near_cols], out_sem.at[1]),
    )
    out_rest = pltpu.make_async_copy(out_v.at[1, :, far_cols], out.at[1, :, far_cols], out_sem.at[2])
    for copy in out_copies:
        copy.start()

    @pl.when(jnp.logical_not(heavy))
    def _():
        out_rest.start()

    for p in (0, 1):
        for j in range(CTX):
            shared(p, j).wait_recv()
    step_q = jnp.concatenate(
        [split_scaled(sq_in[:, h * HEAD_DIM : (h + 1) * HEAD_DIM]) for h in range(GROUP)], axis=0
    )
    width = GROUP * REQS
    request = lax.rem(lax.broadcasted_iota(jnp.int32, (1, width), 1), REQS)
    slot = jnp.zeros((1, width), jnp.int32)
    for r in range(REQS):
        slot = jnp.where(request == r, request_slot[r], slot)
    second = slot == 1
    in_second = second.astype(jnp.bfloat16)
    in_first = (1.0 - second.astype(jnp.float32)).astype(jnp.bfloat16)
    prompts = (owner_slots[0, owner], owner_slots[1, owner])
    p_acc[...] = jnp.zeros_like(p_acc)
    p_top[...] = jnp.full(p_top.shape, FLOOR, jnp.float32)

    def persona_step(i, _):
        scores = []
        for u in range(2):
            j = i * 2 + u
            a = dot_t(twice(kv[prompts[0], j, 0]), step_q)
            b = dot_t(twice(kv[prompts[1], j, 0]), step_q)
            scores.append(jnp.where(second, b, a))
        before = p_top[0:1, :]
        highest = before
        for s in scores:
            highest = jnp.maximum(highest, jnp.max(s, axis=0, keepdims=True))
        total = p_acc[...] * jnp.exp2(before - highest)
        for u in range(2):
            j = i * 2 + u
            w = jnp.exp2(scores[u] - highest).astype(jnp.bfloat16)
            total = total + dot(with_ones(kv[prompts[0], j, 1]), w * in_first)
            total = total + dot(with_ones(kv[prompts[1], j, 1]), w * in_second)
        p_acc[...] = total
        p_top[0:1, :] = highest
        return 0

    lax.fori_loop(0, CTX // 2, persona_step, 0)

    def rows(ref):
        return jnp.concatenate([ref[:, h, :] for h in range(GROUP)], axis=0)

    def spread(row):
        return jnp.broadcast_to(row, (HEAD_DIM, width)).T

    total_p, top_p = spread(p_acc[HEAD_DIM : HEAD_DIM + 1, :]), spread(p_top[0:1, :])
    top_c = rows(c_top)
    highest = jnp.maximum(top_p, top_c)
    weight_p, weight_c = jnp.exp2(top_p - highest), jnp.exp2(top_c - highest)
    mixed = p_acc[:HEAD_DIM, :].T * weight_p + rows(c_out) * weight_c
    mixed = mixed / (total_p * weight_p + rows(c_sum) * weight_c)
    for h in range(GROUP):
        step_v[:, h * HEAD_DIM : (h + 1) * HEAD_DIM] = mixed[h * REQS : (h + 1) * REQS].astype(
            jnp.bfloat16
        )
    step_copy = pltpu.make_async_copy(step_v, step_out, out_sem.at[3])
    step_copy.start()

    for sent in range(N_SENDS):
        move(sent, 0, me, left).wait_send()
    for copy in out_copies:
        copy.wait()
    step_copy.wait()

    @pl.when(heavy)
    def _():
        lend.wait_send()
        give_back.wait_recv()

    @pl.when(jnp.logical_not(heavy))
    def _():
        out_rest.wait()
        give_back.wait_send()


def on_device(pq, pk, pv, sq, ck, cv, lengths, owner_slots, request_slot):
    anywhere = pl.BlockSpec(memory_space=pl.ANY)
    scalars = pl.BlockSpec(memory_space=pltpu.SMEM)
    f32, bf16 = jnp.float32, jnp.bfloat16
    return pl.pallas_call(
        kernel,
        out_shape=(
            jax.ShapeDtypeStruct(pq.shape, bf16),
            jax.ShapeDtypeStruct(sq.shape, bf16),
        ),
        in_specs=[anywhere] * 6 + [scalars] * 3,
        out_specs=(anywhere, anywhere),
        scratch_shapes=[
            pltpu.VMEM((4, CTX, 2, BLOCK, HEAD_DIM), bf16),
            pltpu.VMEM(pq.shape, bf16),
            pltpu.VMEM((BLOCK, HALF * HEAD_DIM), bf16),
            pltpu.VMEM((5, HALF, BLOCK, 2 * HEAD_DIM), bf16),
            pltpu.VMEM((5, HALF, AUG, BLOCK), f32),
            pltpu.VMEM((5, HALF, BLOCK), f32),
            pltpu.VMEM(pq.shape, bf16),
            pltpu.VMEM((BLOCK, HALF * HEAD_DIM), bf16),
            pltpu.VMEM(ck.shape, bf16),
            pltpu.VMEM(cv.shape, bf16),
            pltpu.VMEM(sq.shape, bf16),
            pltpu.VMEM((REQS, GROUP, HEAD_DIM), f32),
            pltpu.VMEM((REQS, GROUP, HEAD_DIM), f32),
            pltpu.VMEM((REQS, GROUP, HEAD_DIM), f32),
            pltpu.VMEM((REQS, GROUP, HEAD_DIM), f32),
            pltpu.VMEM((AUG, GROUP * REQS), f32),
            pltpu.VMEM((8, GROUP * REQS), f32),
            pltpu.VMEM(sq.shape, bf16),
            pltpu.SemaphoreType.DMA((N_SENDS,)),
            pltpu.SemaphoreType.DMA((2, CTX)),
            pltpu.SemaphoreType.DMA((2, CTX)),
            pltpu.SemaphoreType.DMA((4,)),
            pltpu.SemaphoreType.DMA((6,)),
            pltpu.SemaphoreType.DMA((2, REQS // CACHE_GROUP)),
            pltpu.SemaphoreType.DMA((4,)),
        ],
        compiler_params=pltpu.CompilerParams(
            collective_id=0, has_side_effects=True, vmem_limit_bytes=60 << 20
        ),
        cost_estimate=pl.CostEstimate(
            flops=18_000_000_000, bytes_accessed=24 << 20, transcendentals=34_000_000
        ),
        name="prompt_and_step",
    )(pq, pk, pv, sq, ck, cv, lengths, owner_slots.T, request_slot)


def solution(mesh):
    in_specs = (
        P("section", "ctx", "head"),
        P("section", "ctx", "head"),
        P("section", "ctx", "head"),
        P(("section", "ctx"), "head"),
        P(("section", "ctx"), None, "head"),
        P(("section", "ctx"), None, "head"),
        P(("section", "ctx")),
        P(),
        P(("section", "ctx")),
    )
    out_specs = (P("section", "ctx", "head"), P(("section", "ctx"), "head"))
    return jax.shard_map(
        on_device, mesh=mesh, in_specs=in_specs, out_specs=out_specs, check_vma=False
    )
```

```python
import jax
import jax.numpy as jnp
from jax import lax
from jax.experimental import pallas as pl
from jax.experimental.pallas import tpu as pltpu
from jax.sharding import PartitionSpec as P

HEADS = 64
KV_HEADS = 8
HEAD_DIM = 128
GROUP = HEADS // KV_HEADS
FLOOR = -1e30
SCALE2 = 1.4426950408889634 / HEAD_DIM**0.5
MESH = pl.DeviceIdType.MESH
CTX = 8
XS = 4
BLOCK = 512
REQS = 32
MAXC = 1024
CACHE_GROUP = 8
LIMIT = 2.0**100
AUG = HEAD_DIM + 16

HALF = GROUP // 2


N_SENDS = 6 + 2 + 4 + 2 + 16


def dot_t(a, b):
    return lax.dot_general(a, b, (((1,), (1,)), ((), ())), preferred_element_type=jnp.float32)


def dot(a, b):
    return lax.dot_general(a, b, (((1,), (0,)), ((), ())), preferred_element_type=jnp.float32)


def split_scaled(q):
    scaled = q.astype(jnp.float32) * SCALE2
    high = scaled.astype(jnp.bfloat16)
    low = (scaled - high.astype(jnp.float32)).astype(jnp.bfloat16)
    return jnp.concatenate([high, low], axis=1)


def twice(k):
    return jnp.concatenate([k, k], axis=1)


def with_ones(v):
    return jnp.concatenate([v.T, jnp.ones((AUG - HEAD_DIM, v.shape[0]), v.dtype)], axis=0)


def kernel(
    pq, pk, pv, sq, ck, cv, lengths, owner_slots, request_slot,
    out, step_out, kv_out, flag_out,
    kv, q_in, q_split, acc, top, out_v, bad, flag,
    cache_k, cache_v, sq_in, sq_rows,
    c_out, c_top, c_sum, sq_far, p_q, p_slot, p_acc, p_top, step_v,
    send_sem, recv_sem, sib_sem, far_sem, in_sem, cache_sem, out_sem,
):
    section = lax.axis_index("section")
    me = lax.axis_index("ctx")
    y, x = me // XS, lax.rem(me, XS)
    first = section * 2
    lends = me >= CTX - 2
    borrows = jnp.logical_and(y == 0, x >= XS - 2)

    def at(row, col):
        return row * XS + lax.rem(col + XS, XS)

    left, right = at(y, x - 1), at(y, x + 1)
    across, opposite = at(1 - y, x), at(y, x + 2)
    far_left, far_right, far_opposite = at(1 - y, x - 1), at(1 - y, x + 1), at(1 - y, x + 2)

    loads = []
    for p in (0, 1):
        for part, src in ((0, pk), (1, pv)):
            loads.append(
                pltpu.make_async_copy(src.at[p], kv.at[first + p, me, part], in_sem.at[len(loads)])
            )
    loads.append(pltpu.make_async_copy(pq, q_in, in_sem.at[4]))
    loads.append(pltpu.make_async_copy(sq, sq_in, in_sem.at[5]))
    for load in loads:
        load.start()

    def cache_copies(g):
        rows = pl.ds(g * CACHE_GROUP, CACHE_GROUP)
        return (
            pltpu.make_async_copy(ck.at[rows], cache_k.at[rows], cache_sem.at[0, g]),
            pltpu.make_async_copy(cv.at[rows], cache_v.at[rows], cache_sem.at[1, g]),
        )

    for g in range(REQS // CACHE_GROUP):
        for copy in cache_copies(g):
            copy.start()

    barrier = pltpu.get_barrier_semaphore()
    for peer in (left, right, across):
        pl.semaphore_signal(barrier, inc=1, device_id={"ctx": peer}, device_id_type=MESH)
    pl.semaphore_signal(barrier, inc=1, device_id={"section": 1 - section}, device_id_type=MESH)
    pl.semaphore_wait(barrier, 4)

    def move(slot, p, j, to):
        return pltpu.make_async_remote_copy(
            src_ref=kv.at[first + p, j],
            dst_ref=kv.at[first + p, j],
            send_sem=send_sem.at[slot],
            recv_sem=recv_sem.at[p, j],
            device_id={"ctx": to},
            device_id_type=MESH,
        )

    def share(n, p, j):
        return pltpu.make_async_remote_copy(
            src_ref=kv.at[first + p, j],
            dst_ref=kv.at[first + p, j],
            send_sem=send_sem.at[14 + 2 * n + p],
            recv_sem=sib_sem.at[p, j],
            device_id={"section": 1 - section},
            device_id_type=MESH,
        )

    def shared(p, j):
        other = kv.at[2 - first + p, j]
        return pltpu.make_async_remote_copy(
            src_ref=other, dst_ref=other, send_sem=send_sem.at[0], recv_sem=sib_sem.at[p, j],
            device_id={"section": 1 - section}, device_id_type=MESH,
        )

    def far_copy(n, src, dst):
        return pltpu.make_async_remote_copy(
            src_ref=src, dst_ref=dst, send_sem=far_sem.at[n], recv_sem=far_sem.at[4 + n],
            device_id={"ctx": across}, device_id_type=MESH,
        )

    ask = (far_copy(0, sq, sq_far), far_copy(1, p_slot.at[1], p_slot.at[0]))
    answer = (far_copy(2, p_acc.at[0], p_acc.at[1]), far_copy(3, p_top.at[0], p_top.at[1]))

    for p in (0, 1):
        loads[2 * p].wait()
        loads[2 * p + 1].wait()

        move(2 * p + 1, p, me, right).start()
        if p == 0:
            move(2 * p, p, me, left).start()
        move(4 + p, p, me, across).start()

    for p in (0, 1):
        share(0, p, me).start()

    width = GROUP * REQS
    request = lax.rem(lax.broadcasted_iota(jnp.int32, (8, width), 1), REQS)
    slot = jnp.zeros((8, width), jnp.int32)
    for r in range(REQS):
        slot = jnp.where(request == r, request_slot[r], slot)
    p_slot[1] = slot.astype(jnp.float32)

    @pl.when(lends)
    def _():
        for copy in ask:
            copy.start()

    def arrive(p, j):
        move(0, p, j, me).wait_recv()

    def arrives(n, p, j):
        arrive(p, j)
        share(n, p, j).start()

    def first_arrivals():
        arrives(3, 0, across)
        move(8, 0, across, left).start()
        move(2, 1, me, left).start()
        arrives(1, 0, left)
        move(6, 0, left, right).start()
        move(12, 0, left, across).start()
        arrives(2, 0, right)

    def second_arrivals():
        arrives(3, 1, across)
        move(9, 1, across, left).start()
        arrives(1, 1, left)
        move(13, 1, left, across).start()

    def split_step(n, _):
        g, u = n // HALF, lax.rem(n, HALF)
        h = lax.rem(n, GROUP)
        cols = pl.ds(pl.multiple_of(h * HEAD_DIM, HEAD_DIM), HEAD_DIM)
        q_split[g, u] = split_scaled(q_in[g // 2, :, cols])
        return 0

    loads[4].wait()
    lax.fori_loop(0, 4 * HALF, split_step, 0)

    def diagonal_step(p, _):
        keys = twice(kv[first + p, me, 0])
        values = with_ones(kv[first + p, me, 1])
        key_at = lax.broadcasted_iota(jnp.int32, (BLOCK, BLOCK), 0)
        query_at = lax.broadcasted_iota(jnp.int32, (BLOCK, BLOCK), 1)
        scores = [dot_t(keys, q_split[2 * p + h // HALF, h % HALF]) for h in range(GROUP)]
        for h in range(GROUP):
            g, u = 2 * p + h // HALF, h % HALF
            s = jnp.where(key_at <= query_at, scores[h], FLOOR)
            highest = jnp.max(s, axis=0, keepdims=True)
            w = jnp.exp2(s - highest).astype(jnp.bfloat16)
            acc[g, u] = dot(values, w)
            top[g, u : u + 1, :] = highest
        return 0

    lax.fori_loop(0, 2, diagonal_step, 0)


    loads[5].wait()
    for h in range(GROUP):
        sq_rows[:, h, :] = sq_in[:, h * HEAD_DIM : (h + 1) * HEAD_DIM].astype(jnp.float32)

    def cache_step(g, _):
        @pl.when(g == 2)
        def _():
            first_arrivals()

        for copy in cache_copies(g):
            copy.wait()
        scores = []
        for u in range(CACHE_GROUP):
            r = g * CACHE_GROUP + u
            scores.append(dot_t(sq_rows[r].astype(jnp.bfloat16), cache_k[r]))
        for u in range(CACHE_GROUP):
            r = g * CACHE_GROUP + u
            column = lax.broadcasted_iota(jnp.int32, (GROUP, MAXC), 1)
            s = jnp.where(column < lengths[r], scores[u], FLOOR)
            highest = jnp.max(s, axis=1, keepdims=True)
            w = jnp.exp2((s - highest) * SCALE2).astype(jnp.bfloat16)
            total = jnp.sum(w.astype(jnp.float32), axis=1, keepdims=True)
            c_out[r] = dot(w, cache_v[r])
            c_top[r] = jnp.broadcast_to(highest * SCALE2, (GROUP, HEAD_DIM))
            c_sum[r] = jnp.broadcast_to(total, (GROUP, HEAD_DIM))
        return 0

    lax.fori_loop(0, REQS // CACHE_GROUP, cache_step, 0)

    def attend(p, j, tasks):
        keys = twice(kv[first + p, j, 0])
        values = with_ones(kv[first + p, j, 1])
        scores = [dot_t(keys, q_split[g, u]) for g, u in tasks]
        for (g, u), s in zip(tasks, scores):
            w = jnp.exp2(s - top[g, u : u + 1, :]).astype(jnp.bfloat16)
            acc[g, u] += dot(values, w)

    def step_queries(ref):
        return jnp.concatenate(
            [split_scaled(ref[:, h * HEAD_DIM : (h + 1) * HEAD_DIM]) for h in range(GROUP)], axis=0
        )

    p_q[1] = step_queries(sq_in)

    @pl.when(borrows)
    def _():
        for copy in ask:
            copy.wait_recv()
        p_q[0] = step_queries(sq_far)

    def persona_step(n, _):
        t, i = n // (CTX // 2), lax.rem(n, CTX // 2)

        @pl.when(i == 0)
        def _():
            p_acc[t] = jnp.zeros((AUG, width), jnp.float32)
            p_top[t] = jnp.full((8, width), FLOOR, jnp.float32)

        owner = section * CTX + jnp.where(t == 0, across, me)
        prompts = (owner_slots[0, owner], owner_slots[1, owner])
        queries = p_q[t]
        second = p_slot[t, 0:1, :]
        in_second = second.astype(jnp.bfloat16)
        in_first = (1.0 - second).astype(jnp.bfloat16)
        scores = []
        for u in range(2):
            a = dot_t(twice(kv[prompts[0], i * 2 + u, 0]), queries)
            b = dot_t(twice(kv[prompts[1], i * 2 + u, 0]), queries)
            scores.append(jnp.where(second > 0.5, b, a))
        before = p_top[t, 0:1, :]
        highest = before
        for s in scores:
            highest = jnp.maximum(highest, jnp.max(s, axis=0, keepdims=True))
        total = p_acc[t] * jnp.exp2(before - highest)
        for u in range(2):
            w = jnp.exp2(scores[u] - highest).astype(jnp.bfloat16)
            total = total + dot(with_ones(kv[prompts[0], i * 2 + u, 1]), w * in_first)
            total = total + dot(with_ones(kv[prompts[1], i * 2 + u, 1]), w * in_second)
        p_acc[t] = total
        p_top[t, 0:1, :] = highest

        @pl.when(n == CTX // 2 - 1)
        def _():
            for copy in answer:
                copy.start()

        return 0

    bad[...] = jnp.zeros_like(bad)

    def finish(g, u, summed, total):
        cols = pl.ds(pl.multiple_of((lax.rem(g, 2) * HALF + u) * HEAD_DIM, HEAD_DIM), HEAD_DIM)
        out_v[g // 2, :, cols] = (summed * (1.0 / total)).T.astype(jnp.bfloat16)
        bad[...] = jnp.maximum(bad[...], jnp.where(total <= LIMIT, 0.0, 1.0))

    def finish_step(n, _):
        g, u = n // HALF, lax.rem(n, HALF)
        a = acc[g, u]
        finish(g, u, a[:HEAD_DIM], a[HEAD_DIM : HEAD_DIM + 1])
        return 0

    out_copies = [pltpu.make_async_copy(out_v.at[p], out.at[p], out_sem.at[p]) for p in (0, 1)]

    def pick(n, choices):
        j = choices[0]
        for m in range(1, len(choices)):
            j = jnp.where(n == m, choices[m], j)
        return j

    steps = (
        (across, 0), (left, 0), (right, 0), (across, 1), (far_right, 0), (left, 1),
        (far_left, 0), (right, 1), (opposite, 0), (far_left, 1), (far_right, 1),
        (far_opposite, 0), (far_opposite, 1), (opposite, 1),
    )

    def main_step(n, _):
        @pl.when(n == 2)
        def _():
            second_arrivals()

        @pl.when(n == 4)
        def _():
            arrives(6, 0, far_right)

        @pl.when(n == 5)
        def _():
            arrives(5, 0, far_left)
            move(10, 0, far_left, right).start()
            arrives(2, 1, right)
            move(7, 1, right, left).start()

        @pl.when(n == 8)
        def _():
            arrives(4, 0, opposite)

        @pl.when(n == 9)
        def _():
            arrives(5, 1, far_left)
            move(11, 1, far_left, right).start()

        @pl.when(n == 10)
        def _():
            arrives(6, 1, far_right)

        @pl.when(n == 11)
        def _():
            arrives(7, 0, far_opposite)

        @pl.when(n == 12)
        def _():
            lax.fori_loop(0, 2 * HALF, finish_step, 0)
            out_copies[0].start()
            arrives(7, 1, far_opposite)

        @pl.when(n == 13)
        def _():
            arrives(4, 1, opposite)

        j = pick(n, [j for j, _ in steps])
        p = pick(n, [p for _, p in steps])

        @pl.when(j < me)
        def _():
            attend(p, j, [(2 * p + h // HALF, h % HALF) for h in range(GROUP)])

        return 0

    lax.fori_loop(0, len(steps), main_step, 0)
    kv_copy = pltpu.make_async_copy(kv.at[pl.ds(first, 2)], kv_out, out_sem.at[2])
    kv_copy.start()
    lax.fori_loop(2 * HALF, 4 * HALF, finish_step, 0)
    out_copies[1].start()
    highest_bad = jnp.max(jnp.max(bad[...], axis=0, keepdims=True), axis=1, keepdims=True)
    flag[...] = jnp.broadcast_to(highest_bad, flag.shape)
    flag_copy = pltpu.make_async_copy(flag, flag_out, out_sem.at[4])
    flag_copy.start()

    for p in (0, 1):
        for j in range(CTX):
            shared(p, j).wait_recv()
    lax.fori_loop(
        jnp.where(borrows, 0, CTX // 2), jnp.where(lends, CTX // 2, CTX), persona_step, 0
    )

    @pl.when(lends)
    def _():
        for copy in answer:
            copy.wait_recv()

    def rows(ref):
        return jnp.concatenate([ref[:, h, :] for h in range(GROUP)], axis=0)

    def spread(row):
        return jnp.broadcast_to(row, (HEAD_DIM, width)).T

    top_p, top_c = spread(p_top[1, 0:1, :]), rows(c_top)
    highest = jnp.maximum(top_p, top_c)
    weight_p, weight_c = jnp.exp2(top_p - highest), jnp.exp2(top_c - highest)
    total_p = spread(p_acc[1, HEAD_DIM : HEAD_DIM + 1, :])
    mixed = p_acc[1, :HEAD_DIM, :].T * weight_p + rows(c_out) * weight_c
    mixed = mixed / (total_p * weight_p + rows(c_sum) * weight_c)
    for h in range(GROUP):
        step_v[:, h * HEAD_DIM : (h + 1) * HEAD_DIM] = mixed[h * REQS : (h + 1) * REQS].astype(
            jnp.bfloat16
        )
    step_copy = pltpu.make_async_copy(step_v, step_out, out_sem.at[3])
    step_copy.start()

    for sent in range(N_SENDS):
        move(sent, 0, me, left).wait_send()

    @pl.when(lends)
    def _():
        for copy in ask:
            copy.wait_send()

    @pl.when(borrows)
    def _():
        for copy in answer:
            copy.wait_send()

    step_copy.wait()

    for copy in out_copies:
        copy.wait()
    kv_copy.wait()
    flag_copy.wait()


def write_kernel(
    flag, out, step_out, pq, kv, result, step_result,
    held, held_step, q, rows, acc, top, in_sem, out_sem, redo_sem,
):
    pieces = 4
    length = BLOCK // pieces
    pairs = [(step_out, held_step, step_result)]
    for p in (0, 1):
        for n in range(pieces):
            pairs.append([ref.at[p, pl.ds(n * length, length)] for ref in (out, held, result)])
    reads = [pltpu.make_async_copy(a, b, in_sem.at[n]) for n, (a, b, _) in enumerate(pairs)]
    writes = [pltpu.make_async_copy(b, c, out_sem.at[n]) for n, (_, b, c) in enumerate(pairs)]
    for read in reads:
        read.start()
    for read, write in zip(reads, writes):
        read.wait()
        write.start()
    for write in writes:
        write.wait()

    @pl.when(flag[0, 0] > 0.0)
    def _():
        me = lax.axis_index("ctx")
        loads = (
            pltpu.make_async_copy(pq, q, redo_sem.at[0]),
            pltpu.make_async_copy(kv, rows, redo_sem.at[1]),
        )
        for load in loads:
            load.start()
        for load in loads:
            load.wait()

        def head_step(n, _):
            p, h = n // GROUP, lax.rem(n, GROUP)
            cols = pl.ds(pl.multiple_of(h * HEAD_DIM, HEAD_DIM), HEAD_DIM)
            queries = split_scaled(q[p, :, cols])
            acc[...] = jnp.zeros_like(acc)
            top[...] = jnp.full(top.shape, FLOOR, jnp.float32)

            def block_step(i, _):
                j = me - i
                s = dot_t(twice(rows[p, j, 0]), queries)
                key_at = lax.broadcasted_iota(jnp.int32, (BLOCK, BLOCK), 0)
                query_at = lax.broadcasted_iota(jnp.int32, (BLOCK, BLOCK), 1)
                s = jnp.where(key_at - query_at <= i * BLOCK, s, FLOOR)
                before = top[0:1, :]
                highest = jnp.maximum(before, jnp.max(s, axis=0, keepdims=True))
                w = jnp.exp2(s - highest).astype(jnp.bfloat16)
                acc[...] = acc[...] * jnp.exp2(before - highest) + dot(with_ones(rows[p, j, 1]), w)
                top[0:1, :] = highest
                return 0

            lax.fori_loop(0, me + 1, block_step, 0)
            mixed = acc[:HEAD_DIM] * (1.0 / acc[HEAD_DIM : HEAD_DIM + 1])
            held[p, :, cols] = mixed.T.astype(jnp.bfloat16)
            return 0

        lax.fori_loop(0, 2 * GROUP, head_step, 0)
        again = pltpu.make_async_copy(held, result, redo_sem.at[2])
        again.start()
        again.wait()


def write_results(flag, out, step_out, pq, kv):
    anywhere = pl.BlockSpec(memory_space=pl.ANY)
    f32, bf16 = jnp.float32, jnp.bfloat16
    return pl.pallas_call(
        write_kernel,
        out_shape=(
            jax.ShapeDtypeStruct(out.shape, out.dtype),
            jax.ShapeDtypeStruct(step_out.shape, step_out.dtype),
        ),
        in_specs=[pl.BlockSpec(memory_space=pltpu.SMEM)] + [anywhere] * 4,
        out_specs=(anywhere, anywhere),
        scratch_shapes=[
            pltpu.VMEM(out.shape, bf16),
            pltpu.VMEM(step_out.shape, bf16),
            pltpu.VMEM(pq.shape, bf16),
            pltpu.VMEM(kv.shape, bf16),
            pltpu.VMEM((AUG, BLOCK), f32),
            pltpu.VMEM((8, BLOCK), f32),
            pltpu.SemaphoreType.DMA((9,)),
            pltpu.SemaphoreType.DMA((9,)),
            pltpu.SemaphoreType.DMA((3,)),
        ],
        compiler_params=pltpu.CompilerParams(vmem_limit_bytes=60 << 20),
        name="write_results",
    )(flag, out, step_out, pq, kv)


def on_device(pq, pk, pv, sq, ck, cv, lengths, owner_slots, request_slot):
    anywhere = pl.BlockSpec(memory_space=pl.ANY)
    scalars = pl.BlockSpec(memory_space=pltpu.SMEM)
    f32, bf16 = jnp.float32, jnp.bfloat16
    out, step_out, kv, flag = pl.pallas_call(
        kernel,
        out_shape=(
            jax.ShapeDtypeStruct(pq.shape, bf16),
            jax.ShapeDtypeStruct(sq.shape, bf16),
            jax.ShapeDtypeStruct((2, CTX, 2, BLOCK, HEAD_DIM), bf16),
            jax.ShapeDtypeStruct((8, HEAD_DIM), f32),
        ),
        in_specs=[anywhere] * 6 + [scalars] * 3,
        out_specs=(anywhere,) * 4,
        scratch_shapes=[
            pltpu.VMEM((4, CTX, 2, BLOCK, HEAD_DIM), bf16),
            pltpu.VMEM(pq.shape, bf16),
            pltpu.VMEM((4, HALF, BLOCK, 2 * HEAD_DIM), bf16),
            pltpu.VMEM((4, HALF, AUG, BLOCK), f32),
            pltpu.VMEM((4, 8, BLOCK), f32),
            pltpu.VMEM(pq.shape, bf16),
            pltpu.VMEM((8, BLOCK), f32),
            pltpu.VMEM((8, HEAD_DIM), f32),
            pltpu.VMEM(ck.shape, bf16),
            pltpu.VMEM(cv.shape, bf16),
            pltpu.VMEM(sq.shape, bf16),
            pltpu.VMEM((REQS, GROUP, HEAD_DIM), f32),
            pltpu.VMEM((REQS, GROUP, HEAD_DIM), f32),
            pltpu.VMEM((REQS, GROUP, HEAD_DIM), f32),
            pltpu.VMEM((REQS, GROUP, HEAD_DIM), f32),
            pltpu.VMEM(sq.shape, bf16),
            pltpu.VMEM((2, GROUP * REQS, 2 * HEAD_DIM), bf16),
            pltpu.VMEM((2, 8, GROUP * REQS), f32),
            pltpu.VMEM((2, AUG, GROUP * REQS), f32),
            pltpu.VMEM((2, 8, GROUP * REQS), f32),
            pltpu.VMEM(sq.shape, bf16),
            pltpu.SemaphoreType.DMA((N_SENDS,)),
            pltpu.SemaphoreType.DMA((2, CTX)),
            pltpu.SemaphoreType.DMA((2, CTX)),
            pltpu.SemaphoreType.DMA((8,)),
            pltpu.SemaphoreType.DMA((6,)),
            pltpu.SemaphoreType.DMA((2, REQS // CACHE_GROUP)),
            pltpu.SemaphoreType.DMA((5,)),
        ],
        compiler_params=pltpu.CompilerParams(
            collective_id=0, has_side_effects=True, vmem_limit_bytes=60 << 20
        ),
        cost_estimate=pl.CostEstimate(
            flops=18_000_000_000, bytes_accessed=24 << 20, transcendentals=34_000_000
        ),
        name="prompt_and_step",
    )(pq, pk, pv, sq, ck, cv, lengths, owner_slots.T, request_slot)
    return write_results(flag, out, step_out, pq, kv)


def solution(mesh):
    in_specs = (
        P("section", "ctx", "head"),
        P("section", "ctx", "head"),
        P("section", "ctx", "head"),
        P(("section", "ctx"), "head"),
        P(("section", "ctx"), None, "head"),
        P(("section", "ctx"), None, "head"),
        P(("section", "ctx")),
        P(),
        P(("section", "ctx")),
    )
    out_specs = (P("section", "ctx", "head"), P(("section", "ctx"), "head"))
    return jax.shard_map(
        on_device, mesh=mesh, in_specs=in_specs, out_specs=out_specs, check_vma=False
    )
```

```python
import jax
import jax.numpy as jnp
from jax import lax
from jax.experimental import pallas as pl
from jax.experimental.pallas import tpu as pltpu
from jax.sharding import PartitionSpec as P

HEADS = 64
KV_HEADS = 8
HEAD_DIM = 128
GROUP = HEADS // KV_HEADS
FLOOR = -1e30
SCALE2 = 1.4426950408889634 / HEAD_DIM**0.5
MESH = pl.DeviceIdType.MESH
CTX = 8
XS = 4
BLOCK = 512
REQS = 32
MAXC = 1024
CACHE_GROUP = 8
LIMIT = 2.0**100
AUG = HEAD_DIM + 16

HALF = GROUP // 2


N_SENDS = 6 + 2 + 4 + 2 + 16


def dot_t(a, b):
    return lax.dot_general(a, b, (((1,), (1,)), ((), ())), preferred_element_type=jnp.float32)


def dot(a, b):
    return lax.dot_general(a, b, (((1,), (0,)), ((), ())), preferred_element_type=jnp.float32)


def split_scaled(q):
    scaled = q.astype(jnp.float32) * SCALE2
    high = scaled.astype(jnp.bfloat16)
    low = (scaled - high.astype(jnp.float32)).astype(jnp.bfloat16)
    return jnp.concatenate([high, low], axis=1)


def twice(k):
    return jnp.concatenate([k, k], axis=1)


def with_ones(v):
    return jnp.concatenate([v.T, jnp.ones((AUG - HEAD_DIM, v.shape[0]), v.dtype)], axis=0)


def kernel(
    pq, pk, pv, sq, ck, cv, lengths, owner_slots, request_slot,
    out, step_out, kv_out, flag_out,
    kv, q_in, q_split, acc, top, out_v, bad, flag,
    cache_k, cache_v, sq_in, sq_rows,
    c_out, c_top, c_sum, p_q, p_acc, p_top, step_v,
    send_sem, recv_sem, sib_sem, in_sem, cache_sem, out_sem,
):
    section = lax.axis_index("section")
    me = lax.axis_index("ctx")
    y, x = me // XS, lax.rem(me, XS)
    first = section * 2
    owner = section * CTX + me

    def at(row, col):
        return row * XS + lax.rem(col + XS, XS)

    left, right = at(y, x - 1), at(y, x + 1)
    across, opposite = at(1 - y, x), at(y, x + 2)
    far_left, far_right, far_opposite = at(1 - y, x - 1), at(1 - y, x + 1), at(1 - y, x + 2)

    loads = []
    for p in (0, 1):
        for part, src in ((0, pk), (1, pv)):
            loads.append(
                pltpu.make_async_copy(src.at[p], kv.at[first + p, me, part], in_sem.at[len(loads)])
            )
    loads.append(pltpu.make_async_copy(pq, q_in, in_sem.at[4]))
    loads.append(pltpu.make_async_copy(sq, sq_in, in_sem.at[5]))
    for load in loads:
        load.start()

    def cache_copies(g):
        rows = pl.ds(g * CACHE_GROUP, CACHE_GROUP)
        return (
            pltpu.make_async_copy(ck.at[rows], cache_k.at[rows], cache_sem.at[0, g]),
            pltpu.make_async_copy(cv.at[rows], cache_v.at[rows], cache_sem.at[1, g]),
        )

    for g in range(REQS // CACHE_GROUP):
        for copy in cache_copies(g):
            copy.start()

    barrier = pltpu.get_barrier_semaphore()
    for peer in (left, right, across):
        pl.semaphore_signal(barrier, inc=1, device_id={"ctx": peer}, device_id_type=MESH)
    pl.semaphore_signal(barrier, inc=1, device_id={"section": 1 - section}, device_id_type=MESH)
    pl.semaphore_wait(barrier, 4)

    def move(slot, p, j, to):
        return pltpu.make_async_remote_copy(
            src_ref=kv.at[first + p, j],
            dst_ref=kv.at[first + p, j],
            send_sem=send_sem.at[slot],
            recv_sem=recv_sem.at[p, j],
            device_id={"ctx": to},
            device_id_type=MESH,
        )

    def share(n, p, j):
        return pltpu.make_async_remote_copy(
            src_ref=kv.at[first + p, j],
            dst_ref=kv.at[first + p, j],
            send_sem=send_sem.at[14 + 2 * n + p],
            recv_sem=sib_sem.at[p, j],
            device_id={"section": 1 - section},
            device_id_type=MESH,
        )

    def shared(p, j):
        other = kv.at[2 - first + p, j]
        return pltpu.make_async_remote_copy(
            src_ref=other, dst_ref=other, send_sem=send_sem.at[0], recv_sem=sib_sem.at[p, j],
            device_id={"section": 1 - section}, device_id_type=MESH,
        )

    for p in (0, 1):
        loads[2 * p].wait()
        loads[2 * p + 1].wait()

        for n, to in enumerate((right, left)):
            move(2 * p + n, p, me, to).start()
        move(4 + p, p, me, across).start()

    for p in (0, 1):
        share(0, p, me).start()

    def arrive(p, j):
        move(0, p, j, me).wait_recv()

    def arrives(n, p, j):
        arrive(p, j)
        share(n, p, j).start()

    def first_arrivals():
        arrives(3, 0, across)
        move(8, 0, across, left).start()
        arrives(1, 0, left)
        move(6, 0, left, right).start()
        move(12, 0, left, across).start()
        arrives(2, 0, right)

    def second_arrivals():
        arrives(1, 1, left)
        move(13, 1, left, across).start()
        arrives(3, 1, across)
        move(9, 1, across, left).start()
        arrives(2, 1, right)
        move(7, 1, right, left).start()

    def split_step(n, _):
        g, u = n // HALF, lax.rem(n, HALF)
        h = lax.rem(n, GROUP)
        cols = pl.ds(pl.multiple_of(h * HEAD_DIM, HEAD_DIM), HEAD_DIM)
        q_split[g, u] = split_scaled(q_in[g // 2, :, cols])
        return 0

    loads[4].wait()
    lax.fori_loop(0, 4 * HALF, split_step, 0)

    def diagonal_step(p, _):
        keys = twice(kv[first + p, me, 0])
        values = with_ones(kv[first + p, me, 1])
        middle = BLOCK // 2
        key_at = lax.broadcasted_iota(jnp.int32, (middle, BLOCK), 0)
        query_at = lax.broadcasted_iota(jnp.int32, (middle, BLOCK), 1)
        allowed = key_at <= query_at
        tasks = [(2 * p + h // HALF, h % HALF) for h in range(GROUP)]
        first_scores = [dot_t(keys[:middle], q_split[g, u]) for g, u in tasks]
        second_scores = [dot_t(keys[middle:], q_split[g, u, middle:, :]) for g, u in tasks]
        for (g, u), a, b in zip(tasks, first_scores, second_scores):
            a = jnp.where(allowed, a, FLOOR)
            b = jnp.where(allowed[:, :middle], b, FLOOR)
            highest = jnp.max(a, axis=0, keepdims=True)
            late = jnp.maximum(highest[:, middle:], jnp.max(b, axis=0, keepdims=True))
            highest = jnp.concatenate([highest[:, :middle], late], axis=1)
            acc[g, u] = dot(values[:, :middle], jnp.exp2(a - highest).astype(jnp.bfloat16))
            acc[g, u, :, middle:] += dot(values[:, middle:], jnp.exp2(b - late).astype(jnp.bfloat16))
            top[g, u : u + 1, :] = highest
        return 0

    lax.fori_loop(0, 2, diagonal_step, 0)


    loads[5].wait()
    for h in range(GROUP):
        sq_rows[:, h, :] = sq_in[:, h * HEAD_DIM : (h + 1) * HEAD_DIM].astype(jnp.float32)

    def cache_step(g, _):
        for copy in cache_copies(g):
            copy.wait()
        scores = []
        for u in range(CACHE_GROUP):
            r = g * CACHE_GROUP + u
            scores.append(dot_t(sq_rows[r].astype(jnp.bfloat16), cache_k[r]))
        for u in range(CACHE_GROUP):
            r = g * CACHE_GROUP + u
            column = lax.broadcasted_iota(jnp.int32, (GROUP, MAXC), 1)
            s = jnp.where(column < lengths[r], scores[u], FLOOR)
            highest = jnp.max(s, axis=1, keepdims=True)
            w = jnp.exp2((s - highest) * SCALE2).astype(jnp.bfloat16)
            total = jnp.sum(w.astype(jnp.float32), axis=1, keepdims=True)
            c_out[r] = dot(w, cache_v[r])
            c_top[r] = jnp.broadcast_to(highest * SCALE2, (GROUP, HEAD_DIM))
            c_sum[r] = jnp.broadcast_to(total, (GROUP, HEAD_DIM))
        return 0

    lax.fori_loop(0, REQS // CACHE_GROUP, cache_step, 0)
    first_arrivals()

    def attend(p, j, tasks):
        keys = twice(kv[first + p, j, 0])
        values = with_ones(kv[first + p, j, 1])
        scores = [dot_t(keys, q_split[g, u]) for g, u in tasks]
        for (g, u), s in zip(tasks, scores):
            w = jnp.exp2(s - top[g, u : u + 1, :]).astype(jnp.bfloat16)
            acc[g, u] += dot(values, w)

    width = GROUP * REQS
    p_q[...] = jnp.concatenate(
        [split_scaled(sq_in[:, h * HEAD_DIM : (h + 1) * HEAD_DIM]) for h in range(GROUP)], axis=0
    )
    p_acc[...] = jnp.zeros_like(p_acc)
    p_top[...] = jnp.full(p_top.shape, FLOOR, jnp.float32)
    request = lax.rem(lax.broadcasted_iota(jnp.int32, (1, width), 1), REQS)
    slot = jnp.zeros((1, width), jnp.int32)
    for r in range(REQS):
        slot = jnp.where(request == r, request_slot[r], slot)
    in_second = slot.astype(jnp.float32).astype(jnp.bfloat16)
    in_first = (1 - slot).astype(jnp.float32).astype(jnp.bfloat16)
    prompts = (owner_slots[0, owner], owner_slots[1, owner])

    def persona_step(i, _):
        scores = []
        for u in range(2):
            a = dot_t(twice(kv[prompts[0], i * 2 + u, 0]), p_q[...])
            b = dot_t(twice(kv[prompts[1], i * 2 + u, 0]), p_q[...])
            scores.append(jnp.where(slot == 1, b, a))
        before = p_top[0:1, :]
        highest = before
        for s in scores:
            highest = jnp.maximum(highest, jnp.max(s, axis=0, keepdims=True))
        total = p_acc[...] * jnp.exp2(before - highest)
        for u in range(2):
            w = jnp.exp2(scores[u] - highest).astype(jnp.bfloat16)
            total = total + dot(with_ones(kv[prompts[0], i * 2 + u, 1]), w * in_first)
            total = total + dot(with_ones(kv[prompts[1], i * 2 + u, 1]), w * in_second)
        p_acc[...] = total
        p_top[0:1, :] = highest
        return 0

    bad[...] = jnp.zeros_like(bad)

    def finish(g, u, summed, total):
        cols = pl.ds(pl.multiple_of((lax.rem(g, 2) * HALF + u) * HEAD_DIM, HEAD_DIM), HEAD_DIM)
        out_v[g // 2, :, cols] = (summed * (1.0 / total)).T.astype(jnp.bfloat16)
        bad[...] = jnp.maximum(bad[...], jnp.where(total <= LIMIT, 0.0, 1.0))

    def finish_step(n, _):
        g, u = n // HALF, lax.rem(n, HALF)
        a = acc[g, u]
        finish(g, u, a[:HEAD_DIM], a[HEAD_DIM : HEAD_DIM + 1])
        return 0

    out_copies = [pltpu.make_async_copy(out_v.at[p], out.at[p], out_sem.at[p]) for p in (0, 1)]

    def pick(n, choices):
        j = choices[0]
        for m in range(1, len(choices)):
            j = jnp.where(n == m, choices[m], j)
        return j

    steps = (
        (across, 0), (left, 0), (right, 0), (across, 1), (left, 1), (right, 1),
        (opposite, 0), (far_right, 0), (far_left, 0), (far_left, 1), (far_right, 1),
        (far_opposite, 0), (opposite, 1), (far_opposite, 1),
    )

    def main_step(n, _):
        @pl.when(n == 2)
        def _():
            second_arrivals()

        @pl.when(n == 6)
        def _():
            arrives(5, 0, far_left)
            move(10, 0, far_left, right).start()
            arrives(4, 0, opposite)

        @pl.when(n == 7)
        def _():
            arrives(6, 0, far_right)

        @pl.when(n == 8)
        def _():
            arrives(5, 1, far_left)
            move(11, 1, far_left, right).start()

        @pl.when(n == 10)
        def _():
            arrives(6, 1, far_right)

        @pl.when(n == 11)
        def _():
            arrives(7, 0, far_opposite)

        @pl.when(n == 12)
        def _():
            lax.fori_loop(0, 2 * HALF, finish_step, 0)
            out_copies[0].start()
            arrives(4, 1, opposite)

        @pl.when(n == 13)
        def _():
            arrives(7, 1, far_opposite)

        j = pick(n, [j for j, _ in steps])
        p = pick(n, [p for _, p in steps])

        @pl.when(j < me)
        def _():
            attend(p, j, [(2 * p + h // HALF, h % HALF) for h in range(GROUP)])

        return 0

    lax.fori_loop(0, len(steps), main_step, 0)
    kv_copy = pltpu.make_async_copy(kv.at[pl.ds(first, 2)], kv_out, out_sem.at[2])
    kv_copy.start()
    lax.fori_loop(2 * HALF, 4 * HALF, finish_step, 0)
    out_copies[1].start()
    highest_bad = jnp.max(jnp.max(bad[...], axis=0, keepdims=True), axis=1, keepdims=True)
    flag[...] = jnp.broadcast_to(highest_bad, flag.shape)
    flag_copy = pltpu.make_async_copy(flag, flag_out, out_sem.at[4])
    flag_copy.start()

    for p in (0, 1):
        for j in range(CTX):
            shared(p, j).wait_recv()
    lax.fori_loop(0, CTX // 2, persona_step, 0)

    def rows(ref):
        return jnp.concatenate([ref[:, h, :] for h in range(GROUP)], axis=0)

    def spread(row):
        return jnp.broadcast_to(row, (HEAD_DIM, width)).T

    top_p, top_c = spread(p_top[0:1, :]), rows(c_top)
    highest = jnp.maximum(top_p, top_c)
    weight_p, weight_c = jnp.exp2(top_p - highest), jnp.exp2(top_c - highest)
    total_p = spread(p_acc[HEAD_DIM : HEAD_DIM + 1, :])
    mixed = p_acc[:HEAD_DIM, :].T * weight_p + rows(c_out) * weight_c
    mixed = mixed / (total_p * weight_p + rows(c_sum) * weight_c)
    for h in range(GROUP):
        step_v[:, h * HEAD_DIM : (h + 1) * HEAD_DIM] = mixed[h * REQS : (h + 1) * REQS].astype(
            jnp.bfloat16
        )
    step_copy = pltpu.make_async_copy(step_v, step_out, out_sem.at[3])
    step_copy.start()

    for sent in range(N_SENDS):
        move(sent, 0, me, left).wait_send()

    step_copy.wait()

    for copy in out_copies:
        copy.wait()
    kv_copy.wait()
    flag_copy.wait()


def write_kernel(
    flag, out, step_out, pq, kv, result, step_result,
    flag_in, held, held_step, q, rows, acc, top, in_sem, out_sem, redo_sem,
):
    pieces = 4
    length = BLOCK // pieces
    pairs = [(step_out, held_step, step_result)]
    for p in (0, 1):
        for n in range(pieces):
            pairs.append([ref.at[p, pl.ds(n * length, length)] for ref in (out, held, result)])
    reads = [pltpu.make_async_copy(a, b, in_sem.at[n]) for n, (a, b, _) in enumerate(pairs)]
    writes = [pltpu.make_async_copy(b, c, out_sem.at[n]) for n, (_, b, c) in enumerate(pairs)]
    for read in reads:
        read.start()
    flag_read = pltpu.make_async_copy(flag, flag_in, redo_sem.at[3])
    flag_read.start()
    for read, write in zip(reads, writes):
        read.wait()
        write.start()
    for write in writes:
        write.wait()

    flag_read.wait()

    @pl.when(flag_in[0, 0] > 0.0)
    def _():
        me = lax.axis_index("ctx")
        loads = (
            pltpu.make_async_copy(pq, q, redo_sem.at[0]),
            pltpu.make_async_copy(kv, rows, redo_sem.at[1]),
        )
        for load in loads:
            load.start()
        for load in loads:
            load.wait()

        def head_step(n, _):
            p, h = n // GROUP, lax.rem(n, GROUP)
            cols = pl.ds(pl.multiple_of(h * HEAD_DIM, HEAD_DIM), HEAD_DIM)
            queries = split_scaled(q[p, :, cols])
            acc[...] = jnp.zeros_like(acc)
            top[...] = jnp.full(top.shape, FLOOR, jnp.float32)

            def block_step(i, _):
                j = me - i
                s = dot_t(twice(rows[p, j, 0]), queries)
                key_at = lax.broadcasted_iota(jnp.int32, (BLOCK, BLOCK), 0)
                query_at = lax.broadcasted_iota(jnp.int32, (BLOCK, BLOCK), 1)
                s = jnp.where(key_at - query_at <= i * BLOCK, s, FLOOR)
                before = top[0:1, :]
                highest = jnp.maximum(before, jnp.max(s, axis=0, keepdims=True))
                w = jnp.exp2(s - highest).astype(jnp.bfloat16)
                acc[...] = acc[...] * jnp.exp2(before - highest) + dot(with_ones(rows[p, j, 1]), w)
                top[0:1, :] = highest
                return 0

            lax.fori_loop(0, me + 1, block_step, 0)
            mixed = acc[:HEAD_DIM] * (1.0 / acc[HEAD_DIM : HEAD_DIM + 1])
            held[p, :, cols] = mixed.T.astype(jnp.bfloat16)
            return 0

        lax.fori_loop(0, 2 * GROUP, head_step, 0)
        again = pltpu.make_async_copy(held, result, redo_sem.at[2])
        again.start()
        again.wait()


def write_results(flag, out, step_out, pq, kv):
    anywhere = pl.BlockSpec(memory_space=pl.ANY)
    f32, bf16 = jnp.float32, jnp.bfloat16
    return pl.pallas_call(
        write_kernel,
        out_shape=(
            jax.ShapeDtypeStruct(out.shape, out.dtype),
            jax.ShapeDtypeStruct(step_out.shape, step_out.dtype),
        ),
        in_specs=[anywhere] * 5,
        out_specs=(anywhere, anywhere),
        scratch_shapes=[
            pltpu.SMEM(flag.shape, f32),
            pltpu.VMEM(out.shape, bf16),
            pltpu.VMEM(step_out.shape, bf16),
            pltpu.VMEM(pq.shape, bf16),
            pltpu.VMEM(kv.shape, bf16),
            pltpu.VMEM((AUG, BLOCK), f32),
            pltpu.VMEM((8, BLOCK), f32),
            pltpu.SemaphoreType.DMA((9,)),
            pltpu.SemaphoreType.DMA((9,)),
            pltpu.SemaphoreType.DMA((4,)),
        ],
        compiler_params=pltpu.CompilerParams(vmem_limit_bytes=60 << 20),
        name="write_results",
    )(flag, out, step_out, pq, kv)


def on_device(pq, pk, pv, sq, ck, cv, lengths, owner_slots, request_slot):
    anywhere = pl.BlockSpec(memory_space=pl.ANY)
    scalars = pl.BlockSpec(memory_space=pltpu.SMEM)
    f32, bf16 = jnp.float32, jnp.bfloat16
    out, step_out, kv, flag = pl.pallas_call(
        kernel,
        out_shape=(
            jax.ShapeDtypeStruct(pq.shape, bf16),
            jax.ShapeDtypeStruct(sq.shape, bf16),
            jax.ShapeDtypeStruct((2, CTX, 2, BLOCK, HEAD_DIM), bf16),
            jax.ShapeDtypeStruct((8, HEAD_DIM), f32),
        ),
        in_specs=[anywhere] * 6 + [scalars] * 3,
        out_specs=(anywhere,) * 4,
        scratch_shapes=[
            pltpu.VMEM((4, CTX, 2, BLOCK, HEAD_DIM), bf16),
            pltpu.VMEM(pq.shape, bf16),
            pltpu.VMEM((4, HALF, BLOCK, 2 * HEAD_DIM), bf16),
            pltpu.VMEM((4, HALF, AUG, BLOCK), f32),
            pltpu.VMEM((4, 8, BLOCK), f32),
            pltpu.VMEM(pq.shape, bf16),
            pltpu.VMEM((8, BLOCK), f32),
            pltpu.VMEM((8, HEAD_DIM), f32),
            pltpu.VMEM(ck.shape, bf16),
            pltpu.VMEM(cv.shape, bf16),
            pltpu.VMEM(sq.shape, bf16),
            pltpu.VMEM((REQS, GROUP, HEAD_DIM), f32),
            pltpu.VMEM((REQS, GROUP, HEAD_DIM), f32),
            pltpu.VMEM((REQS, GROUP, HEAD_DIM), f32),
            pltpu.VMEM((REQS, GROUP, HEAD_DIM), f32),
            pltpu.VMEM((GROUP * REQS, 2 * HEAD_DIM), bf16),
            pltpu.VMEM((AUG, GROUP * REQS), f32),
            pltpu.VMEM((8, GROUP * REQS), f32),
            pltpu.VMEM(sq.shape, bf16),
            pltpu.SemaphoreType.DMA((N_SENDS,)),
            pltpu.SemaphoreType.DMA((2, CTX)),
            pltpu.SemaphoreType.DMA((2, CTX)),
            pltpu.SemaphoreType.DMA((6,)),
            pltpu.SemaphoreType.DMA((2, REQS // CACHE_GROUP)),
            pltpu.SemaphoreType.DMA((5,)),
        ],
        compiler_params=pltpu.CompilerParams(
            collective_id=0, has_side_effects=True, vmem_limit_bytes=60 << 20
        ),
        cost_estimate=pl.CostEstimate(
            flops=18_000_000_000, bytes_accessed=24 << 20, transcendentals=34_000_000
        ),
        name="prompt_and_step",
    )(pq, pk, pv, sq, ck, cv, lengths, owner_slots.T, request_slot)
    return write_results(flag, out, step_out, pq, kv)


def solution(mesh):
    in_specs = (
        P("section", "ctx", "head"),
        P("section", "ctx", "head"),
        P("section", "ctx", "head"),
        P(("section", "ctx"), "head"),
        P(("section", "ctx"), None, "head"),
        P(("section", "ctx"), None, "head"),
        P(("section", "ctx")),
        P(),
        P(("section", "ctx")),
    )
    out_specs = (P("section", "ctx", "head"), P(("section", "ctx"), "head"))
    return jax.shard_map(
        on_device, mesh=mesh, in_specs=in_specs, out_specs=out_specs, check_vma=False
    )
```

```python
import jax
import jax.numpy as jnp
from jax import lax
from jax.experimental import pallas as pl
from jax.experimental.pallas import tpu as pltpu
from jax.sharding import PartitionSpec as P

HEADS = 64
KV_HEADS = 8
HEAD_DIM = 128
GROUP = HEADS // KV_HEADS
FLOOR = -1e30
SCALE2 = 1.4426950408889634 / HEAD_DIM**0.5
MESH = pl.DeviceIdType.MESH
CTX = 8
XS = 4
BLOCK = 512
REQS = 32
MAXC = 1024
CACHE_GROUP = 8
LIMIT = 2.0**100
AUG = HEAD_DIM + 16

HALF = GROUP // 2


N_SENDS = 6 + 2 + 4 + 2 + 16


def dot_t(a, b):
    return lax.dot_general(a, b, (((1,), (1,)), ((), ())), preferred_element_type=jnp.float32)


def dot(a, b):
    return lax.dot_general(a, b, (((1,), (0,)), ((), ())), preferred_element_type=jnp.float32)


def split_scaled(q):
    scaled = q.astype(jnp.float32) * SCALE2
    high = scaled.astype(jnp.bfloat16)
    low = (scaled - high.astype(jnp.float32)).astype(jnp.bfloat16)
    return jnp.concatenate([high, low], axis=1)


def twice(k):
    return jnp.concatenate([k, k], axis=1)


def with_ones(v):
    return jnp.concatenate([v.T, jnp.ones((AUG - HEAD_DIM, v.shape[0]), v.dtype)], axis=0)


def kernel(
    pq, pk, pv, sq, ck, cv, lengths, owner_slots, request_slot,
    out, step_out, kv_out, flag_out,
    kv, q_in, q_split, acc, top, out_v, bad, flag,
    cache_k, cache_v, sq_in, sq_rows,
    c_out, c_top, c_sum, sq_far, p_q, p_slot, p_acc, p_top, step_v,
    send_sem, recv_sem, sib_sem, far_sem, in_sem, cache_sem, out_sem,
):
    section = lax.axis_index("section")
    me = lax.axis_index("ctx")
    y, x = me // XS, lax.rem(me, XS)
    first = section * 2
    lends = me >= CTX - 2
    borrows = jnp.logical_and(y == 0, x >= XS - 2)

    def at(row, col):
        return row * XS + lax.rem(col + XS, XS)

    left, right = at(y, x - 1), at(y, x + 1)
    across, opposite = at(1 - y, x), at(y, x + 2)
    far_left, far_right, far_opposite = at(1 - y, x - 1), at(1 - y, x + 1), at(1 - y, x + 2)

    loads = []
    for p in (0, 1):
        for part, src in ((0, pk), (1, pv)):
            loads.append(
                pltpu.make_async_copy(src.at[p], kv.at[first + p, me, part], in_sem.at[len(loads)])
            )
    loads.append(pltpu.make_async_copy(pq, q_in, in_sem.at[4]))
    loads.append(pltpu.make_async_copy(sq, sq_in, in_sem.at[5]))
    for load in loads:
        load.start()

    def cache_copies(g):
        rows = pl.ds(g * CACHE_GROUP, CACHE_GROUP)
        return (
            pltpu.make_async_copy(ck.at[rows], cache_k.at[rows], cache_sem.at[0, g]),
            pltpu.make_async_copy(cv.at[rows], cache_v.at[rows], cache_sem.at[1, g]),
        )

    for g in range(REQS // CACHE_GROUP):
        for copy in cache_copies(g):
            copy.start()

    barrier = pltpu.get_barrier_semaphore()
    for peer in (left, right, across):
        pl.semaphore_signal(barrier, inc=1, device_id={"ctx": peer}, device_id_type=MESH)
    pl.semaphore_signal(barrier, inc=1, device_id={"section": 1 - section}, device_id_type=MESH)
    pl.semaphore_wait(barrier, 4)

    def move(slot, p, j, to):
        return pltpu.make_async_remote_copy(
            src_ref=kv.at[first + p, j],
            dst_ref=kv.at[first + p, j],
            send_sem=send_sem.at[slot],
            recv_sem=recv_sem.at[p, j],
            device_id={"ctx": to},
            device_id_type=MESH,
        )

    def share(n, p, j):
        return pltpu.make_async_remote_copy(
            src_ref=kv.at[first + p, j],
            dst_ref=kv.at[first + p, j],
            send_sem=send_sem.at[14 + 2 * n + p],
            recv_sem=sib_sem.at[p, j],
            device_id={"section": 1 - section},
            device_id_type=MESH,
        )

    def shared(p, j):
        other = kv.at[2 - first + p, j]
        return pltpu.make_async_remote_copy(
            src_ref=other, dst_ref=other, send_sem=send_sem.at[0], recv_sem=sib_sem.at[p, j],
            device_id={"section": 1 - section}, device_id_type=MESH,
        )

    def far_copy(n, src, dst):
        return pltpu.make_async_remote_copy(
            src_ref=src, dst_ref=dst, send_sem=far_sem.at[n], recv_sem=far_sem.at[4 + n],
            device_id={"ctx": across}, device_id_type=MESH,
        )

    ask = (far_copy(0, sq, sq_far), far_copy(1, p_slot.at[1], p_slot.at[0]))
    answer = (far_copy(2, p_acc.at[0], p_acc.at[1]), far_copy(3, p_top.at[0], p_top.at[1]))

    for p in (0, 1):
        loads[2 * p].wait()
        loads[2 * p + 1].wait()

        for n, to in enumerate((right, left)):
            move(2 * p + n, p, me, to).start()
        move(4 + p, p, me, across).start()

    for p in (0, 1):
        share(0, p, me).start()

    width = GROUP * REQS
    request = lax.rem(lax.broadcasted_iota(jnp.int32, (8, width), 1), REQS)
    slot = jnp.zeros((8, width), jnp.int32)
    for r in range(REQS):
        slot = jnp.where(request == r, request_slot[r], slot)
    p_slot[1] = slot.astype(jnp.float32)

    @pl.when(lends)
    def _():
        for copy in ask:
            copy.start()

    def arrive(p, j):
        move(0, p, j, me).wait_recv()

    def arrives(n, p, j):
        arrive(p, j)
        share(n, p, j).start()

    def first_arrivals():
        arrives(3, 0, across)
        move(8, 0, across, left).start()
        arrives(1, 0, left)
        move(6, 0, left, right).start()
        move(12, 0, left, across).start()
        arrives(2, 0, right)

    def second_arrivals():
        arrives(1, 1, left)
        move(13, 1, left, across).start()
        arrives(3, 1, across)
        move(9, 1, across, left).start()
        arrives(2, 1, right)
        move(7, 1, right, left).start()

    def split_step(n, _):
        g, u = n // HALF, lax.rem(n, HALF)
        h = lax.rem(n, GROUP)
        cols = pl.ds(pl.multiple_of(h * HEAD_DIM, HEAD_DIM), HEAD_DIM)
        q_split[g, u] = split_scaled(q_in[g // 2, :, cols])
        return 0

    loads[4].wait()
    lax.fori_loop(0, 4 * HALF, split_step, 0)

    def diagonal_step(p, _):
        keys = twice(kv[first + p, me, 0])
        values = with_ones(kv[first + p, me, 1])
        middle = BLOCK // 2
        key_at = lax.broadcasted_iota(jnp.int32, (middle, BLOCK), 0)
        query_at = lax.broadcasted_iota(jnp.int32, (middle, BLOCK), 1)
        allowed = key_at <= query_at
        tasks = [(2 * p + h // HALF, h % HALF) for h in range(GROUP)]
        first_scores = [dot_t(keys[:middle], q_split[g, u]) for g, u in tasks]
        second_scores = [dot_t(keys[middle:], q_split[g, u, middle:, :]) for g, u in tasks]
        for (g, u), a, b in zip(tasks, first_scores, second_scores):
            a = jnp.where(allowed, a, FLOOR)
            b = jnp.where(allowed[:, :middle], b, FLOOR)
            highest = jnp.max(a, axis=0, keepdims=True)
            late = jnp.maximum(highest[:, middle:], jnp.max(b, axis=0, keepdims=True))
            highest = jnp.concatenate([highest[:, :middle], late], axis=1)
            acc[g, u] = dot(values[:, :middle], jnp.exp2(a - highest).astype(jnp.bfloat16))
            acc[g, u, :, middle:] += dot(values[:, middle:], jnp.exp2(b - late).astype(jnp.bfloat16))
            top[g, u : u + 1, :] = highest
        return 0

    lax.fori_loop(0, 2, diagonal_step, 0)


    loads[5].wait()
    for h in range(GROUP):
        sq_rows[:, h, :] = sq_in[:, h * HEAD_DIM : (h + 1) * HEAD_DIM].astype(jnp.float32)

    def cache_step(g, _):
        for copy in cache_copies(g):
            copy.wait()
        scores = []
        for u in range(CACHE_GROUP):
            r = g * CACHE_GROUP + u
            scores.append(dot_t(sq_rows[r].astype(jnp.bfloat16), cache_k[r]))
        for u in range(CACHE_GROUP):
            r = g * CACHE_GROUP + u
            column = lax.broadcasted_iota(jnp.int32, (GROUP, MAXC), 1)
            s = jnp.where(column < lengths[r], scores[u], FLOOR)
            highest = jnp.max(s, axis=1, keepdims=True)
            w = jnp.exp2((s - highest) * SCALE2).astype(jnp.bfloat16)
            total = jnp.sum(w.astype(jnp.float32), axis=1, keepdims=True)
            c_out[r] = dot(w, cache_v[r])
            c_top[r] = jnp.broadcast_to(highest * SCALE2, (GROUP, HEAD_DIM))
            c_sum[r] = jnp.broadcast_to(total, (GROUP, HEAD_DIM))
        return 0

    lax.fori_loop(0, REQS // CACHE_GROUP, cache_step, 0)
    first_arrivals()

    def attend(p, j, tasks):
        keys = twice(kv[first + p, j, 0])
        values = with_ones(kv[first + p, j, 1])
        scores = [dot_t(keys, q_split[g, u]) for g, u in tasks]
        for (g, u), s in zip(tasks, scores):
            w = jnp.exp2(s - top[g, u : u + 1, :]).astype(jnp.bfloat16)
            acc[g, u] += dot(values, w)

    def step_queries(ref):
        return jnp.concatenate(
            [split_scaled(ref[:, h * HEAD_DIM : (h + 1) * HEAD_DIM]) for h in range(GROUP)], axis=0
        )

    p_q[1] = step_queries(sq_in)

    def persona_step(n, _):
        t, i = n // (CTX // 2), lax.rem(n, CTX // 2)

        @pl.when(i == 0)
        def _():
            p_acc[t] = jnp.zeros((AUG, width), jnp.float32)
            p_top[t] = jnp.full((8, width), FLOOR, jnp.float32)

        owner = section * CTX + jnp.where(t == 0, across, me)
        prompts = (owner_slots[0, owner], owner_slots[1, owner])
        queries = p_q[t]
        second = p_slot[t, 0:1, :]
        in_second = second.astype(jnp.bfloat16)
        in_first = (1.0 - second).astype(jnp.bfloat16)
        scores = []
        for u in range(2):
            a = dot_t(twice(kv[prompts[0], i * 2 + u, 0]), queries)
            b = dot_t(twice(kv[prompts[1], i * 2 + u, 0]), queries)
            scores.append(jnp.where(second > 0.5, b, a))
        before = p_top[t, 0:1, :]
        highest = before
        for s in scores:
            highest = jnp.maximum(highest, jnp.max(s, axis=0, keepdims=True))
        total = p_acc[t] * jnp.exp2(before - highest)
        for u in range(2):
            w = jnp.exp2(scores[u] - highest).astype(jnp.bfloat16)
            total = total + dot(with_ones(kv[prompts[0], i * 2 + u, 1]), w * in_first)
            total = total + dot(with_ones(kv[prompts[1], i * 2 + u, 1]), w * in_second)
        p_acc[t] = total
        p_top[t, 0:1, :] = highest

        @pl.when(n == CTX // 2 - 1)
        def _():
            for copy in answer:
                copy.start()

        return 0

    bad[...] = jnp.zeros_like(bad)

    def finish(g, u, summed, total):
        cols = pl.ds(pl.multiple_of((lax.rem(g, 2) * HALF + u) * HEAD_DIM, HEAD_DIM), HEAD_DIM)
        out_v[g // 2, :, cols] = (summed * (1.0 / total)).T.astype(jnp.bfloat16)
        bad[...] = jnp.maximum(bad[...], jnp.where(total <= LIMIT, 0.0, 1.0))

    def finish_step(n, _):
        g, u = n // HALF, lax.rem(n, HALF)
        a = acc[g, u]
        finish(g, u, a[:HEAD_DIM], a[HEAD_DIM : HEAD_DIM + 1])
        return 0

    out_copies = [pltpu.make_async_copy(out_v.at[p], out.at[p], out_sem.at[p]) for p in (0, 1)]

    def pick(n, choices):
        j = choices[0]
        for m in range(1, len(choices)):
            j = jnp.where(n == m, choices[m], j)
        return j

    steps = (
        (across, 0), (left, 0), (right, 0), (across, 1), (left, 1), (right, 1),
        (opposite, 0), (far_right, 0), (far_left, 0), (far_left, 1), (far_right, 1),
        (far_opposite, 0), (opposite, 1), (far_opposite, 1),
    )

    def main_step(n, _):
        @pl.when(n == 2)
        def _():
            second_arrivals()

        @pl.when(n == 5)
        def _():
            arrives(5, 0, far_left)
            move(10, 0, far_left, right).start()

        @pl.when(n == 6)
        def _():
            arrives(4, 0, opposite)

        @pl.when(n == 7)
        def _():
            arrives(6, 0, far_right)

        @pl.when(n == 7)
        def _():
            arrives(5, 1, far_left)
            move(11, 1, far_left, right).start()

        @pl.when(n == 10)
        def _():
            arrives(6, 1, far_right)

        @pl.when(n == 11)
        def _():
            arrives(7, 0, far_opposite)

        @pl.when(n == 12)
        def _():
            lax.fori_loop(0, 2 * HALF, finish_step, 0)
            out_copies[0].start()
            arrives(4, 1, opposite)

        @pl.when(n == 13)
        def _():
            arrives(7, 1, far_opposite)

        j = pick(n, [j for j, _ in steps])
        p = pick(n, [p for _, p in steps])

        @pl.when(j < me)
        def _():
            attend(p, j, [(2 * p + h // HALF, h % HALF) for h in range(GROUP)])

        return 0

    lax.fori_loop(0, len(steps), main_step, 0)
    kv_copy = pltpu.make_async_copy(kv.at[pl.ds(first, 2)], kv_out, out_sem.at[2])
    kv_copy.start()
    lax.fori_loop(2 * HALF, 4 * HALF, finish_step, 0)
    out_copies[1].start()
    highest_bad = jnp.max(jnp.max(bad[...], axis=0, keepdims=True), axis=1, keepdims=True)
    flag[...] = jnp.broadcast_to(highest_bad, flag.shape)
    flag_copy = pltpu.make_async_copy(flag, flag_out, out_sem.at[4])
    flag_copy.start()

    for p in (0, 1):
        for j in range(CTX):
            shared(p, j).wait_recv()
    @pl.when(borrows)
    def _():
        for copy in ask:
            copy.wait_recv()
        p_q[0] = step_queries(sq_far)

    lax.fori_loop(
        jnp.where(borrows, 0, CTX // 2), jnp.where(lends, CTX // 2, CTX), persona_step, 0
    )

    @pl.when(lends)
    def _():
        for copy in answer:
            copy.wait_recv()

    def rows(ref):
        return jnp.concatenate([ref[:, h, :] for h in range(GROUP)], axis=0)

    def spread(row):
        return jnp.broadcast_to(row, (HEAD_DIM, width)).T

    top_p, top_c = spread(p_top[1, 0:1, :]), rows(c_top)
    highest = jnp.maximum(top_p, top_c)
    weight_p, weight_c = jnp.exp2(top_p - highest), jnp.exp2(top_c - highest)
    total_p = spread(p_acc[1, HEAD_DIM : HEAD_DIM + 1, :])
    mixed = p_acc[1, :HEAD_DIM, :].T * weight_p + rows(c_out) * weight_c
    mixed = mixed / (total_p * weight_p + rows(c_sum) * weight_c)
    for h in range(GROUP):
        step_v[:, h * HEAD_DIM : (h + 1) * HEAD_DIM] = mixed[h * REQS : (h + 1) * REQS].astype(
            jnp.bfloat16
        )
    step_copy = pltpu.make_async_copy(step_v, step_out, out_sem.at[3])
    step_copy.start()

    for sent in range(N_SENDS):
        move(sent, 0, me, left).wait_send()

    @pl.when(lends)
    def _():
        for copy in ask:
            copy.wait_send()

    @pl.when(borrows)
    def _():
        for copy in answer:
            copy.wait_send()

    step_copy.wait()

    for copy in out_copies:
        copy.wait()
    kv_copy.wait()
    flag_copy.wait()


def write_kernel(
    flag, out, step_out, pq, kv, result, step_result,
    flag_in, held, held_step, q, rows, acc, top, in_sem, out_sem, redo_sem,
):
    pieces = 4
    length = BLOCK // pieces
    pairs = [(step_out, held_step, step_result)]
    for p in (0, 1):
        for n in range(pieces):
            pairs.append([ref.at[p, pl.ds(n * length, length)] for ref in (out, held, result)])
    reads = [pltpu.make_async_copy(a, b, in_sem.at[n]) for n, (a, b, _) in enumerate(pairs)]
    writes = [pltpu.make_async_copy(b, c, out_sem.at[n]) for n, (_, b, c) in enumerate(pairs)]
    for read in reads:
        read.start()
    flag_read = pltpu.make_async_copy(flag, flag_in, redo_sem.at[3])
    flag_read.start()
    for read, write in zip(reads, writes):
        read.wait()
        write.start()
    for write in writes:
        write.wait()

    flag_read.wait()

    @pl.when(flag_in[0, 0] > 0.0)
    def _():
        me = lax.axis_index("ctx")
        loads = (
            pltpu.make_async_copy(pq, q, redo_sem.at[0]),
            pltpu.make_async_copy(kv, rows, redo_sem.at[1]),
        )
        for load in loads:
            load.start()
        for load in loads:
            load.wait()

        def head_step(n, _):
            p, h = n // GROUP, lax.rem(n, GROUP)
            cols = pl.ds(pl.multiple_of(h * HEAD_DIM, HEAD_DIM), HEAD_DIM)
            queries = split_scaled(q[p, :, cols])
            acc[...] = jnp.zeros_like(acc)
            top[...] = jnp.full(top.shape, FLOOR, jnp.float32)

            def block_step(i, _):
                j = me - i
                s = dot_t(twice(rows[p, j, 0]), queries)
                key_at = lax.broadcasted_iota(jnp.int32, (BLOCK, BLOCK), 0)
                query_at = lax.broadcasted_iota(jnp.int32, (BLOCK, BLOCK), 1)
                s = jnp.where(key_at - query_at <= i * BLOCK, s, FLOOR)
                before = top[0:1, :]
                highest = jnp.maximum(before, jnp.max(s, axis=0, keepdims=True))
                w = jnp.exp2(s - highest).astype(jnp.bfloat16)
                acc[...] = acc[...] * jnp.exp2(before - highest) + dot(with_ones(rows[p, j, 1]), w)
                top[0:1, :] = highest
                return 0

            lax.fori_loop(0, me + 1, block_step, 0)
            mixed = acc[:HEAD_DIM] * (1.0 / acc[HEAD_DIM : HEAD_DIM + 1])
            held[p, :, cols] = mixed.T.astype(jnp.bfloat16)
            return 0

        lax.fori_loop(0, 2 * GROUP, head_step, 0)
        again = pltpu.make_async_copy(held, result, redo_sem.at[2])
        again.start()
        again.wait()


def write_results(flag, out, step_out, pq, kv):
    anywhere = pl.BlockSpec(memory_space=pl.ANY)
    f32, bf16 = jnp.float32, jnp.bfloat16
    return pl.pallas_call(
        write_kernel,
        out_shape=(
            jax.ShapeDtypeStruct(out.shape, out.dtype),
            jax.ShapeDtypeStruct(step_out.shape, step_out.dtype),
        ),
        in_specs=[anywhere] * 5,
        out_specs=(anywhere, anywhere),
        scratch_shapes=[
            pltpu.SMEM(flag.shape, f32),
            pltpu.VMEM(out.shape, bf16),
            pltpu.VMEM(step_out.shape, bf16),
            pltpu.VMEM(pq.shape, bf16),
            pltpu.VMEM(kv.shape, bf16),
            pltpu.VMEM((AUG, BLOCK), f32),
            pltpu.VMEM((8, BLOCK), f32),
            pltpu.SemaphoreType.DMA((9,)),
            pltpu.SemaphoreType.DMA((9,)),
            pltpu.SemaphoreType.DMA((4,)),
        ],
        compiler_params=pltpu.CompilerParams(vmem_limit_bytes=60 << 20),
        name="write_results",
    )(flag, out, step_out, pq, kv)


def on_device(pq, pk, pv, sq, ck, cv, lengths, owner_slots, request_slot):
    anywhere = pl.BlockSpec(memory_space=pl.ANY)
    scalars = pl.BlockSpec(memory_space=pltpu.SMEM)
    f32, bf16 = jnp.float32, jnp.bfloat16
    out, step_out, kv, flag = pl.pallas_call(
        kernel,
        out_shape=(
            jax.ShapeDtypeStruct(pq.shape, bf16),
            jax.ShapeDtypeStruct(sq.shape, bf16),
            jax.ShapeDtypeStruct((2, CTX, 2, BLOCK, HEAD_DIM), bf16),
            jax.ShapeDtypeStruct((8, HEAD_DIM), f32),
        ),
        in_specs=[anywhere] * 6 + [scalars] * 3,
        out_specs=(anywhere,) * 4,
        scratch_shapes=[
            pltpu.VMEM((4, CTX, 2, BLOCK, HEAD_DIM), bf16),
            pltpu.VMEM(pq.shape, bf16),
            pltpu.VMEM((4, HALF, BLOCK, 2 * HEAD_DIM), bf16),
            pltpu.VMEM((4, HALF, AUG, BLOCK), f32),
            pltpu.VMEM((4, 8, BLOCK), f32),
            pltpu.VMEM(pq.shape, bf16),
            pltpu.VMEM((8, BLOCK), f32),
            pltpu.VMEM((8, HEAD_DIM), f32),
            pltpu.VMEM(ck.shape, bf16),
            pltpu.VMEM(cv.shape, bf16),
            pltpu.VMEM(sq.shape, bf16),
            pltpu.VMEM((REQS, GROUP, HEAD_DIM), f32),
            pltpu.VMEM((REQS, GROUP, HEAD_DIM), f32),
            pltpu.VMEM((REQS, GROUP, HEAD_DIM), f32),
            pltpu.VMEM((REQS, GROUP, HEAD_DIM), f32),
            pltpu.VMEM(sq.shape, bf16),
            pltpu.VMEM((2, GROUP * REQS, 2 * HEAD_DIM), bf16),
            pltpu.VMEM((2, 8, GROUP * REQS), f32),
            pltpu.VMEM((2, AUG, GROUP * REQS), f32),
            pltpu.VMEM((2, 8, GROUP * REQS), f32),
            pltpu.VMEM(sq.shape, bf16),
            pltpu.SemaphoreType.DMA((N_SENDS,)),
            pltpu.SemaphoreType.DMA((2, CTX)),
            pltpu.SemaphoreType.DMA((2, CTX)),
            pltpu.SemaphoreType.DMA((8,)),
            pltpu.SemaphoreType.DMA((6,)),
            pltpu.SemaphoreType.DMA((2, REQS // CACHE_GROUP)),
            pltpu.SemaphoreType.DMA((5,)),
        ],
        compiler_params=pltpu.CompilerParams(
            collective_id=0, has_side_effects=True, vmem_limit_bytes=60 << 20
        ),
        cost_estimate=pl.CostEstimate(
            flops=18_000_000_000, bytes_accessed=24 << 20, transcendentals=34_000_000
        ),
        name="prompt_and_step",
    )(pq, pk, pv, sq, ck, cv, lengths, owner_slots.T, request_slot)
    return write_results(flag, out, step_out, pq, kv)


def solution(mesh):
    in_specs = (
        P("section", "ctx", "head"),
        P("section", "ctx", "head"),
        P("section", "ctx", "head"),
        P(("section", "ctx"), "head"),
        P(("section", "ctx"), None, "head"),
        P(("section", "ctx"), None, "head"),
        P(("section", "ctx")),
        P(),
        P(("section", "ctx")),
    )
    out_specs = (P("section", "ctx", "head"), P(("section", "ctx"), "head"))
    return jax.shard_map(
        on_device, mesh=mesh, in_specs=in_specs, out_specs=out_specs, check_vma=False
    )
```
